32 devices in a mesh: groups: 2 (over y), pairs: 8 (over z, x), rows: 2 (over core).
Axes of the slice: x: 2, y: 2, z: 4, core: 2. Of those that a mesh axis runs over, the one named last changes fastest.
Arguments:
- first_image: float32 [16, 128, 256], P(('groups', 'pairs'), 'rows'), parts along dimension 0, may hold values from -12 to 12
- second_image: float32 [16, 128, 256], P(('groups', 'pairs'), 'rows'), parts along dimension 0, may hold values from -12 to 12
- prior_motion: float32 [2, 16, 128, 256], P(None, ('groups', 'pairs'), 'rows'), parts along dimension 1, may hold values from -40 to 40
- offsets: int32 [64, 2], replicated, may hold values from -4 to 4, as said below
- pair_epochs: int32 [16, 2], P('groups'), parts along dimension 0, may hold values from 0 to 128, as said below
- pair_slot: int32 [16], P('groups'), parts along dimension 0, may hold values from 0 to 7, each once
Outputs:
- velocity: float32 [2, 128, 4, 16384], P(None, None, ('groups', 'rows'), 'pairs'), parts along dimension 2
- motion: float32 [2, 16, 128, 256], P(None, ('groups', 'pairs'), 'rows'), parts along dimension 1
The draws below stay inside these ranges and needn't reach their ends.
There are 2 independent parts, one for each index of `groups`. The reference program is written for one: setup_inputs(seed, part) draws one part's arguments, and reference() takes and returns one part's arrays. A program takes and returns all parts, laid end to end along the dimension named above; an argument that names none is the same for every part. Nothing has to cross between parts.
Inputs may be any that keep to these rules, and one draw needn't show every extreme that they name: 64 distinct offsets; every offset with a component of magnitude 4 is among them. `pair_epochs`: each row has first < after. `pair_slot`: a permutation of the pairs.
All inputs are finite; a program needn't handle non-finite values. Where the reference program divides by a largest or mean magnitude, that divisor is 1e-20 or more.
Results may differ from the reference program's by a relative error of at most 0.0003.
Values sent between devices are 32-bit elements; how exact they have to be, the bound alone decides.
A program may use at most 64 MiB of HBM per device.

```python
import jax
import jax.numpy as jnp
from jax import lax

OFFSETS = 64
SEARCH = 4
RADIUS = 4
EPOCHS = 128
RB = 64
W = 256
ITERS = 4
ROUNDS = 2
PAIRS = 8
H = 128
N_ROWS = 2


def image_pair(key):
    subkeys = jax.random.split(jax.random.fold_in(key, 7), 4)
    border = 4
    texture = jax.random.normal(subkeys[0], (PAIRS, H + 2 * border, W + 2 * border), jnp.float32)
    lower_log = jnp.log(0.1)
    upper_log = jnp.log(1.5)
    contrast = jnp.exp(jax.random.uniform(subkeys[1], (PAIRS, H // 8 + 1, W // 8 + 1), jnp.float32, lower_log, upper_log))
    contrast = jnp.repeat(jnp.repeat(contrast, 8, axis=1), 8, axis=2)[:, :H, :W]
    shifts = jax.random.randint(subkeys[2], (PAIRS, 2), -3, 4).astype(jnp.int32)
    moved = jax.vmap(lambda plane, row_shift, col_shift: lax.dynamic_slice(plane, (border + row_shift, border + col_shift), (H, W)))(texture, shifts[:, 0], shifts[:, 1])
    jitter = jax.random.normal(subkeys[3], (PAIRS, H, W), jnp.float32)
    first_window = texture[:, border:border + H, border:border + W] * contrast
    second_view = (moved + 0.5 * jitter) * contrast
    return (jnp.clip(first_window, -12.0, 12.0), jnp.clip(second_view, -12.0, 12.0))


def draw_first_image(key, part):
    return image_pair(key)[0]


def draw_second_image(key, part):
    return image_pair(key)[1]


def draw_prior_motion(key, part):
    subkeys = jax.random.split(jax.random.fold_in(key, 23), 1)
    gentle = jnp.clip(3.0 * jax.random.normal(subkeys[0], (2, PAIRS, H, W), jnp.float32), -9.0, 9.0)
    return gentle


def draw_offsets(key, part):
    subkeys = jax.random.split(jax.random.fold_in(key, 31), 2)
    grid_side = 2 * SEARCH + 1
    item_count = jnp.arange(grid_side * grid_side, dtype=jnp.int32)
    row_part = item_count // grid_side - SEARCH
    col_part = item_count % grid_side - SEARCH
    border_cell = (jnp.abs(row_part) == SEARCH) | (jnp.abs(col_part) == SEARCH)
    ranking = jax.random.permutation(subkeys[0], grid_side * grid_side).astype(jnp.int32)
    priority = jnp.where(border_cell, ranking - grid_side * grid_side, ranking)
    chosen = jnp.argsort(priority, stable=True)[:OFFSETS]
    chosen = chosen[jax.random.permutation(subkeys[1], OFFSETS)]
    return jnp.stack((row_part[chosen], col_part[chosen]), axis=1).astype(jnp.int32)


def draw_pair_epochs(key, part):
    subkeys = jax.random.split(jax.random.fold_in(key, 41), 2)
    starts = jax.random.randint(subkeys[0], (PAIRS,), 0, EPOCHS - 1).astype(jnp.int32)
    lengths_drawn = jax.random.randint(subkeys[1], (PAIRS,), 1, EPOCHS // 4 + 1).astype(jnp.int32)
    starts = starts.at[0].set(0)
    finishes = jnp.minimum(starts + lengths_drawn, EPOCHS)
    finishes = finishes.at[PAIRS - 1].set(EPOCHS)
    return jnp.stack((starts, finishes), axis=1).astype(jnp.int32)


def setup_inputs(seed: int = 0, part: int = 0) -> dict:
    streams_of = jax.random.split(jax.random.key(seed), 7)
    part_splits = jax.random.split(jax.random.fold_in(streams_of[6], part), 7)
    first_image = draw_first_image(jax.random.fold_in(jax.random.fold_in(streams_of[6], part), 71), part)
    second_image = draw_second_image(jax.random.fold_in(jax.random.fold_in(streams_of[6], part), 71), part)
    prior_motion = draw_prior_motion(jax.random.fold_in(jax.random.fold_in(streams_of[6], part), 71), part)
    offsets = draw_offsets(jax.random.fold_in(streams_of[6], 71), part)
    pair_epochs = draw_pair_epochs(jax.random.fold_in(jax.random.fold_in(streams_of[6], part), 71), part)
    pair_slot = jax.random.permutation(part_splits[5], PAIRS).astype(jnp.int32)
    return {"first_image": first_image, "second_image": second_image, "prior_motion": prior_motion, "offsets": offsets, "pair_epochs": pair_epochs, "pair_slot": pair_slot}


SOFTMIN_HEAT = 0.1
PRIOR_STRENGTH = 0.05
PENALTY = 4.0
SPARSITY = 0.4
VARIANCE_FLOOR = 0.05
HIGHEST = lax.Precision.HIGHEST
NEWTON_STEPS = 32

def invert_normal(normal_matrix):
    order = normal_matrix.shape[0]
    identity = jnp.eye(order, dtype=jnp.float32)
    column_bound = jnp.max(lax.optimization_barrier(jnp.sum(jnp.abs(normal_matrix), axis=0)))
    estimate = identity / column_bound
    for step in range(NEWTON_STEPS):
        product = jnp.dot(normal_matrix, estimate, precision=HIGHEST)
        estimate = jnp.dot(estimate, 2.0 * identity - product, precision=HIGHEST)
    return estimate

def box_sum(values):
    window = 2 * RADIUS + 1
    height = values.shape[-2] - 2 * RADIUS
    breadth = values.shape[-1] - 2 * RADIUS
    running = values[..., 0:height, :]
    for position in range(1, window):
        running = running + values[..., position:position + height, :]
    summed = running[..., 0:breadth]
    for position in range(1, window):
        summed = summed + running[..., position:position + breadth]
    return summed / float(window * window)

def correlate(shift_vector, first_padded, second_padded, mean_first, var_first, mean_second_all, square_second_all, height, columns):
    row_start = shift_vector[0] + SEARCH
    col_start = shift_vector[1] + SEARCH
    mean_second = lax.dynamic_slice(mean_second_all, (row_start, col_start), (height, columns))
    square_second = lax.dynamic_slice(square_second_all, (row_start, col_start), (height, columns))
    window_second = lax.dynamic_slice(second_padded, (row_start, col_start), (height + 2 * RADIUS, columns + 2 * RADIUS))
    covariance = box_sum(first_padded * window_second) - mean_first * mean_second
    var_second = square_second - mean_second * mean_second
    return covariance / jnp.sqrt(jnp.maximum(var_first, VARIANCE_FLOOR) * jnp.maximum(var_second, VARIANCE_FLOOR))

def match_pair(first_pair, second_pair, prior_pair, offsets):
    margin = SEARCH + RADIUS
    height, columns = first_pair.shape
    first_padded = jnp.pad(first_pair, RADIUS)
    second_padded = jnp.pad(second_pair, margin)
    mean_first = box_sum(first_padded)
    var_first = box_sum(first_padded * first_padded) - mean_first * mean_first
    mean_second_all = box_sum(second_padded)
    square_second_all = box_sum(second_padded * second_padded)
    cross_correlation = jax.vmap(lambda shift_vector: correlate(shift_vector, first_padded, second_padded, mean_first, var_first, mean_second_all, square_second_all, height, columns))(offsets)
    shifts = offsets.astype(jnp.float32)
    pixel_distance = (shifts[:, 0, None, None] - prior_pair[0]) ** 2 + (shifts[:, 1, None, None] - prior_pair[1]) ** 2
    match_scores = (cross_correlation - PRIOR_STRENGTH * pixel_distance) / SOFTMIN_HEAT
    weights = jax.nn.softmax(match_scores, axis=0)
    return jnp.stack((lax.optimization_barrier(jnp.sum(weights * shifts[:, 0, None, None], axis=0)), lax.optimization_barrier(jnp.sum(weights * shifts[:, 1, None, None], axis=0))))

def build_design(pair_epochs, pair_slot):
    pair_number = jnp.arange(pair_slot.shape[0], dtype=jnp.int32)
    chooser = (pair_slot[:, None] == pair_number[None, :]).astype(jnp.int32)
    starts = lax.optimization_barrier(jnp.sum(chooser * pair_epochs[None, :, 0], axis=1))
    finishes = lax.optimization_barrier(jnp.sum(chooser * pair_epochs[None, :, 1], axis=1))
    epoch_number = jnp.arange(EPOCHS, dtype=jnp.int32)
    inside = (epoch_number[None, :] >= starts[:, None]) & (epoch_number[None, :] < finishes[:, None])
    return inside.astype(jnp.float32)

def reference(first_image, second_image, prior_motion, offsets, pair_epochs, pair_slot):
    design_matrix = build_design(pair_epochs, pair_slot)
    normal_matrix = jnp.dot(design_matrix.T, design_matrix, precision=HIGHEST) + PENALTY * jnp.eye(EPOCHS, dtype=jnp.float32)
    inverse_matrix = invert_normal(normal_matrix)
    threshold = SPARSITY / PENALTY
    sparse = jnp.zeros((2, EPOCHS, H * W), jnp.float32)
    scaled = jnp.zeros((2, EPOCHS, H * W), jnp.float32)
    prior_field = prior_motion
    motion = prior_motion
    for round_number in range(ROUNDS):
        matched = lax.map(lambda members: match_pair(members[0], members[1], members[2], offsets), (first_image, second_image, jnp.moveaxis(prior_field, 1, 0)))
        motion = jnp.moveaxis(matched, 0, 1)
        observed = motion.reshape(2, PAIRS, H * W)
        fixed_part = jnp.einsum('pe,cpn->cen', design_matrix, observed, precision=HIGHEST)
        for iteration in range(ITERS):
            target = fixed_part + PENALTY * (sparse - scaled)
            estimate = jnp.einsum('ef,cfn->cen', inverse_matrix, target, precision=HIGHEST)
            blended = estimate + scaled
            sparse = blended - jnp.clip(blended, -threshold, threshold)
            scaled = blended - sparse
        if round_number + 1 < ROUNDS:
            predicted = jnp.einsum('pe,cen->cpn', design_matrix, sparse, precision=HIGHEST).reshape(2, PAIRS, H, W)
            prior_field = 0.5 * (prior_motion + predicted)
    return (sparse.reshape(2, EPOCHS, N_ROWS, RB * W), motion)
```

```python
import functools

import jax
import jax.numpy as jnp
from jax import lax
from jax.experimental import pallas as pl
from jax.experimental.pallas import tpu as pltpu
from jax.sharding import PartitionSpec as P

SEARCH = 4
RADIUS = 4
EPOCHS = 128
ITERS = 4
ROUNDS = 2

SOFTMIN_HEAT = 0.1
PRIOR_STRENGTH = 0.05
PENALTY = 4.0
SPARSITY = 0.4
VARIANCE_FLOOR = 0.05
HIGHEST = lax.Precision.HIGHEST

SIDE = 2 * SEARCH + 1
WINDOW = 2 * RADIUS + 1
MARGIN = SEARCH + RADIUS
SUB = 8
LANES = 128
AREA = 1.0 / float(WINDOW * WINDOW)
VMEM_BYTES = 40 * 1024 * 1024
BLOCK = 4


def vmem_spec():
    return pl.BlockSpec(memory_space=pltpu.VMEM)


def smem_spec():
    return pl.BlockSpec(memory_space=pltpu.SMEM)


def params(**more):
    return pltpu.CompilerParams(vmem_limit_bytes=VMEM_BYTES, **more)


def parts_of(values):
    high = values.astype(jnp.bfloat16)
    rest = values - high.astype(jnp.float32)
    middle = rest.astype(jnp.bfloat16)
    low = (rest - middle.astype(jnp.float32)).astype(jnp.bfloat16)
    return high, middle, low


def band_matrix(columns, shift):
    row = lax.broadcasted_iota(jnp.int32, (columns, columns), 0)
    col = lax.broadcasted_iota(jnp.int32, (columns, columns), 1)
    return (jnp.abs(row - col - shift) <= RADIUS).astype(jnp.float32).astype(jnp.bfloat16)


def column_box(values, band):
    high, middle, low = parts_of(values)
    mm = functools.partial(jnp.dot, preferred_element_type=jnp.float32)
    return mm(high, band) + (mm(middle, band) + mm(low, band))


def row_box(planes, count):
    result = []
    for base in range(0, count, SUB):
        mid = base + WINDOW - 2
        suffix = {mid: planes[mid]}
        for i in range(mid - 1, base - 1, -1):
            suffix[i] = planes[i] + suffix[i + 1]
        prefix = {mid + 1: planes[mid + 1]}
        for i in range(mid + 2, base + SUB - 1 + WINDOW):
            prefix[i] = prefix[i - 1] + planes[i]
        for i in range(base, base + SUB):
            result.append(suffix[i] + prefix[i + WINDOW - 1])
    return result


def inverse_root(values):
    guess = lax.rsqrt(values)
    return guess * (1.5 - 0.5 * values * guess * guess)


def split_lanes(values):
    return jnp.stack([values[:, i : i + LANES] for i in range(0, values.shape[1], LANES)])


def strided(ref, start, stride):
    rows = pl.ds(start, SUB, stride=stride)
    return jnp.concatenate([ref[i, rows, :] for i in range(ref.shape[0])], axis=-1)


def store_strided(ref, start, stride, values):
    rows = pl.ds(start, SUB, stride=stride)
    for i in range(ref.shape[0]):
        ref[i, rows, :] = values[:, i * LANES : (i + 1) * LANES]


def prepare(image_ref, first_ref, second_ref, f_ref, s_ref, mean_ref, inv_ref, mean1_ref, inv1_ref):
    rows, columns = first_ref.shape[0] - 2 * MARGIN, first_ref.shape[1]
    steps = rows // SUB
    band = band_matrix(columns, 0)

    image_ref[0] = split_lanes(first_ref[...])
    image_ref[1] = split_lanes(second_ref[...])
    raw = [strided(image_ref.at[0], SEARCH + t, steps) for t in range(steps + 2 * RADIUS)]
    scaled = [x * AREA for x in raw]
    for t, x in enumerate(scaled):
        f_ref[t] = x
    sums = row_box(scaled, steps) + row_box([a * b for a, b in zip(raw, scaled)], steps)
    boxed = column_box(jnp.concatenate(sums, axis=0), band)
    mean1 = boxed[:rows]
    var1 = boxed[rows:] - mean1 * mean1
    mean1_ref[...] = mean1.reshape(steps, SUB, columns)
    inv1 = inverse_root(jnp.maximum(var1, VARIANCE_FLOOR)) * (1.0 / SOFTMIN_HEAT)
    inv1_ref[...] = inv1.reshape(steps, SUB, columns)

    reach = steps + 2 * MARGIN
    second = [strided(image_ref.at[1], t, steps) for t in range(reach)]
    wide = steps + 2 * SEARCH
    sums = row_box(second, wide) + row_box([x * x for x in second], wide)
    sums = parts_of(jnp.concatenate(sums, axis=0))
    stacked = jnp.concatenate(second, axis=0)
    lane = lax.broadcasted_iota(jnp.int32, stacked.shape, 1)
    half = wide * SUB
    for place in range(SIDE):
        shift = place - SEARCH
        moved = pltpu.roll(stacked, (-shift) % columns, 1) if shift else stacked
        inside = (lane + shift >= 0) & (lane + shift < columns)
        s_ref[place] = jnp.where(inside, moved, 0.0).reshape(reach, SUB, columns)
        shifted_band = band_matrix(columns, shift)
        mm = functools.partial(jnp.dot, preferred_element_type=jnp.float32)
        boxed = mm(sums[0], shifted_band) + (
            mm(sums[1], shifted_band) + mm(sums[2], shifted_band)
        )
        boxed = boxed * AREA
        mean = boxed[:half]
        var = boxed[half:] - mean * mean
        mean_ref[place] = mean.reshape(wide, SUB, columns)
        inv = inverse_root(jnp.maximum(var, VARIANCE_FLOOR))
        inv_ref[place] = inv.reshape(wide, SUB, columns)


def correlate(offsets_ref, f_ref, s_ref, mean_ref, inv_ref, mean1_ref, inv1_ref, e_ref):
    steps, _, columns = mean1_ref.shape
    rows = steps * SUB
    band = band_matrix(columns, 0)
    count = offsets_ref.shape[0]
    block = BLOCK if count % BLOCK == 0 else 1

    def body(number, carry):
        sums = []
        for i in range(block):
            k = number * block + i
            oy = offsets_ref[k, 0] + SEARCH
            ox = offsets_ref[k, 1] + SEARCH
            planes = [f_ref[t] * s_ref[ox, oy + t] for t in range(steps + 2 * RADIUS)]
            sums += row_box(planes, steps)
        boxed = column_box(jnp.concatenate(sums, axis=0), band)
        for i in range(block):
            k = number * block + i
            oy = offsets_ref[k, 0] + SEARCH
            ox = offsets_ref[k, 1] + SEARCH
            for t in range(steps):
                at = i * rows + t * SUB
                cov = boxed[at : at + SUB] - mean1_ref[t] * mean_ref[ox, oy + t]
                e_ref[k, t] = jnp.exp(cov * (inv1_ref[t] * inv_ref[ox, oy + t]))
        return carry

    lax.fori_loop(0, count // block, body, 0)


def match(offsets_ref, e_ref, prior_row, prior_col, a_ref, b_ref, store):
    count, steps = e_ref.shape[:2]
    curve = 0.5 * (2.0 * PRIOR_STRENGTH / SOFTMIN_HEAT)
    for t in range(steps):
        for ref, prior in ((a_ref, prior_row(t)), (b_ref, prior_col(t))):
            near = jnp.clip(jnp.floor(prior + 0.5), -float(SEARCH), float(SEARCH))
            twice = near - 2.0 * prior
            for place in range(SIDE):
                i = float(place - SEARCH)
                ref[place, t] = jnp.exp(curve * ((near - i) * (twice + i)))
    together = 2
    for base in range(0, steps, together):
        zero = jnp.zeros((together,) + e_ref.shape[2:], jnp.float32)

        def body(k, carry):
            total, rows, cols = carry
            oy = offsets_ref[k, 0]
            ox = offsets_ref[k, 1]
            here = pl.ds(base, together)
            weight = e_ref[k, here] * (a_ref[oy + SEARCH, here] * b_ref[ox + SEARCH, here])
            return (
                total + weight,
                rows + weight * oy.astype(jnp.float32),
                cols + weight * ox.astype(jnp.float32),
            )

        total, rows, cols = lax.fori_loop(0, count, body, (zero, zero, zero), unroll=8)
        for i in range(together):
            store(base + i, rows[i] / total[i], cols[i] / total[i])


def design_kernel(epochs_ref, slot_ref, coef_ref, seg_ref, ends_ref):
    pairs = slot_ref.shape[0]
    ends = 2 * pairs
    row_id = lax.broadcasted_iota(jnp.int32, (pairs, pairs), 0)
    col_id = lax.broadcasted_iota(jnp.int32, (pairs, pairs), 1)
    end_id = lax.broadcasted_iota(jnp.int32, (ends, pairs), 0)
    end_col = lax.broadcasted_iota(jnp.int32, (ends, pairs), 1)
    seg_id = lax.broadcasted_iota(jnp.int32, (ends, EPOCHS), 0)
    epoch = lax.broadcasted_iota(jnp.int32, (ends, EPOCHS), 1)

    def gather(j, state):
        first_r, after_r, first_c, after_c, mark, mark_e, first_e, after_e = state
        first = epochs_ref[slot_ref[j], 0]
        after = epochs_ref[slot_ref[j], 1]
        ends_ref[0, j] = first
        ends_ref[1, j] = after
        return (
            jnp.where(row_id == j, first, first_r),
            jnp.where(row_id == j, after, after_r),
            jnp.where(col_id == j, first, first_c),
            jnp.where(col_id == j, after, after_c),
            jnp.where(end_id == j, first, jnp.where(end_id == j + pairs, after, mark)),
            jnp.where(seg_id == j, first, jnp.where(seg_id == j + pairs, after, mark_e)),
            jnp.where(end_col == j, first, first_e),
            jnp.where(end_col == j, after, after_e),
        )

    square = jnp.zeros((pairs, pairs), jnp.int32)
    tall = jnp.zeros((ends, pairs), jnp.int32)
    state = (square, square, square, square, tall, jnp.zeros((ends, EPOCHS), jnp.int32), tall, tall)
    first_r, after_r, first_c, after_c, mark, mark_e, first_e, after_e = lax.fori_loop(
        0, pairs, gather, state
    )
    overlap = jnp.maximum(jnp.minimum(after_r, after_c) - jnp.maximum(first_r, first_c), 0)
    matrix = overlap.astype(jnp.float32) + jnp.where(row_id == col_id, PENALTY, 0.0)

    def eliminate(j, a):
        on_row = row_id == j
        on_col = col_id == j
        row = jnp.sum(jnp.where(on_row, a, 0.0), axis=0, keepdims=True)
        col = jnp.sum(jnp.where(on_col, a, 0.0), axis=1, keepdims=True)
        pivot = jnp.sum(jnp.where(col_id[:1] == j, row, 0.0), axis=1, keepdims=True)
        scale = 1.0 / pivot
        inner = a - col * (row * scale)
        return jnp.where(
            on_row,
            jnp.where(on_col, scale, row * scale),
            jnp.where(on_col, -col * scale, inner),
        )

    inverse = lax.fori_loop(0, pairs, eliminate, matrix)
    inside = ((mark >= first_e) & (mark < after_e)).astype(jnp.float32)
    coef_ref[...] = jnp.dot(
        inside, inverse, precision=HIGHEST, preferred_element_type=jnp.float32
    )
    latest = jnp.max(jnp.where(mark_e <= epoch, mark_e, -1), axis=0, keepdims=True)
    which = jnp.max(jnp.where(mark_e == latest, seg_id, -1), axis=0, keepdims=True)
    seg_ref[...] = jnp.where(latest < 0, ends, which)


def design(pair_epochs, pair_slot):
    pairs = pair_slot.shape[0]
    return pl.pallas_call(
        design_kernel,
        out_shape=(
            jax.ShapeDtypeStruct((2 * pairs, pairs), jnp.float32),
            jax.ShapeDtypeStruct((1, EPOCHS), jnp.int32),
            jax.ShapeDtypeStruct((2, pairs), jnp.int32),
        ),
        in_specs=[smem_spec(), smem_spec()],
        out_specs=(vmem_spec(), vmem_spec(), smem_spec()),
        compiler_params=params(),
        name="design",
    )(pair_epochs, pair_slot)


def invert(coef_ref, seg_ref, ends_ref, d_ref, before, z_ref, g_ref, t_ref, cum_ref, predicted):
    pairs = d_ref.shape[1]
    ends = 2 * pairs
    threshold = SPARSITY / PENALTY
    plane = (2,) + d_ref.shape[2:]
    zero = jnp.zeros(plane, jnp.float32)
    t_ref[ends] = zero
    cum_ref[0] = zero
    short = pairs <= 16

    def pair_loop(count, body):
        if short:
            for j in range(count):
                body(j)
        else:
            pl.loop(0, count)(body)

    for iteration in range(ITERS):
        start = before is None and iteration == 0
        z_from, g_from = before if before and iteration == 0 else (z_ref, g_ref)
        last = iteration + 1 == ITERS and predicted is not None

        def residual(p):
            return d_ref[:, p] if start else d_ref[:, p] - g_from[:, p]

        if short:
            gaps = [residual(p) for p in range(pairs)]
            for j in range(ends):
                value = coef_ref[j, 0] * gaps[0]
                for p in range(1, pairs):
                    value = value + coef_ref[j, p] * gaps[p]
                t_ref[j] = value
        else:

            def fill(j):
                t_ref[j] = lax.fori_loop(
                    0, pairs, lambda p, v: v + coef_ref[j, p] * residual(p), zero
                )

            pl.loop(0, ends)(fill)

        def epoch_step(e, carry):
            s = t_ref[seg_ref[0, e]]
            if not start:
                s = s + z_from[:, e]
            u = jnp.clip(s, -threshold, threshold)
            z = s - u
            z_ref[:, e] = z
            run = carry[0] + (z - u)
            cum_ref[e + 1] = run
            if not last:
                return (run,)
            run_z = carry[1] + z
            predicted[1][e + 1] = run_z
            return (run, run_z)

        lax.fori_loop(0, EPOCHS, epoch_step, (zero, zero) if last else (zero,), unroll=8)

        def collect(p):
            first, after = ends_ref[0, p], ends_ref[1, p]
            g_ref[:, p] = cum_ref[after] - cum_ref[first]
            if last:
                predicted[0][:, p] = predicted[1][after] - predicted[1][first]

        pair_loop(pairs, collect)


def match_scratch(steps, columns):
    plane = (SUB, columns)
    extended = (2, columns // LANES, steps * SUB + 2 * MARGIN, LANES)
    return [
        pltpu.VMEM(extended, jnp.float32),
        pltpu.VMEM((steps + 2 * RADIUS,) + plane, jnp.float32),
        pltpu.VMEM((SIDE, steps + 2 * MARGIN) + plane, jnp.float32),
        pltpu.VMEM((SIDE, steps + 2 * SEARCH) + plane, jnp.float32),
        pltpu.VMEM((SIDE, steps + 2 * SEARCH) + plane, jnp.float32),
        pltpu.VMEM((steps,) + plane, jnp.float32),
        pltpu.VMEM((steps,) + plane, jnp.float32),
    ]


def weight_scratch(steps, columns):
    tables = [pltpu.VMEM((SIDE, steps, SUB, columns), jnp.float32)] * 2
    return tables + [pltpu.VMEM((2, columns // LANES, steps * SUB, LANES), jnp.float32)]


def match_on(offsets_ref, e_ref, prior_ref, back_ref, a_ref, b_ref, field_ref, motion_ref):
    steps = e_ref.shape[1]
    for component in range(2):
        values = prior_ref[component]
        if back_ref is not None:
            values = 0.5 * (values + back_ref[component])
        field_ref[component] = split_lanes(values)

    def prior(component):
        return lambda t: strided(field_ref.at[component], t, steps)

    def store(t, row, col):
        store_strided(field_ref.at[0], t, steps, row)
        store_strided(field_ref.at[1], t, steps, col)

    match(offsets_ref, e_ref, prior(0), prior(1), a_ref, b_ref, store)
    for component in range(2):
        halves = [field_ref[component, i] for i in range(field_ref.shape[1])]
        motion_ref[component] = jnp.concatenate(halves, axis=-1)


def first_kernel(offsets_ref, images_ref, prior_ref, e_ref, motion_ref, *scratch):
    image_ref, *tables = scratch[:7]
    prepare(image_ref, images_ref.at[0], images_ref.at[1], *tables)
    correlate(offsets_ref, *tables, e_ref)
    match_on(offsets_ref, e_ref, prior_ref, None, *scratch[7:], motion_ref)


def again_kernel(offsets_ref, e_ref, prior_ref, back_ref, motion_ref, *scratch):
    match_on(offsets_ref, e_ref, prior_ref, back_ref, *scratch, motion_ref)


def invert_first_kernel(coef_ref, seg_ref, ends_ref, d_ref, z_ref, g_ref, gz_ref, t_ref, cum_ref, cumz_ref):
    cumz_ref[0] = jnp.zeros(cumz_ref.shape[1:], jnp.float32)
    invert(coef_ref, seg_ref, ends_ref, d_ref, None, z_ref, g_ref, t_ref, cum_ref, (gz_ref, cumz_ref))


def invert_last_kernel(coef_ref, seg_ref, ends_ref, d_ref, zin_ref, gin_ref, z_ref, g_ref, t_ref, cum_ref):
    invert(coef_ref, seg_ref, ends_ref, d_ref, (zin_ref, gin_ref), z_ref, g_ref, t_ref, cum_ref, None)


def with_halo(cells, axis, dim, width):
    count = lax.axis_size(axis)
    head = lax.slice_in_dim(cells, 0, width, axis=dim)
    tail = lax.slice_in_dim(cells, cells.shape[dim] - width, cells.shape[dim], axis=dim)
    down = lax.ppermute(tail, axis, [(i, i + 1) for i in range(count - 1)])
    up = lax.ppermute(head, axis, [(i + 1, i) for i in range(count - 1)])
    return jnp.concatenate([down, cells, up], axis=dim)


def per_device(first_image, second_image, prior_motion, offsets, pair_epochs, pair_slot):
    rows, columns = first_image.shape[1:]
    steps = rows // SUB
    pairs = lax.axis_size("pairs")
    pixels = rows * columns // pairs
    fold = (pixels // LANES, LANES) if pixels % LANES == 0 else (1, pixels)
    f32 = functools.partial(jax.ShapeDtypeStruct, dtype=jnp.float32)
    prior = prior_motion[:, 0]
    coef, seg, ends = design(pair_epochs, pair_slot)
    images = with_halo(jnp.concatenate((first_image, second_image), axis=0), "rows", 1, MARGIN)
    e, motion = pl.pallas_call(
        first_kernel,
        out_shape=(f32((offsets.shape[0], steps, SUB, columns)), f32((2, rows, columns))),
        in_specs=[smem_spec(), vmem_spec(), vmem_spec()],
        out_specs=(vmem_spec(), vmem_spec()),
        scratch_shapes=match_scratch(steps, columns) + weight_scratch(steps, columns),
        compiler_params=params(),
        name="correlate",
    )(offsets, images, prior)

    def spread(field):
        outgoing = field.reshape(2, 1, pairs, pixels)
        arrived = lax.all_to_all(outgoing, "pairs", split_axis=2, concat_axis=1, tiled=True)
        return arrived.reshape((2, pairs) + fold)

    def collect(field):
        outgoing = field.reshape(2, pairs, 1, pixels)
        arrived = lax.all_to_all(outgoing, "pairs", split_axis=1, concat_axis=2, tiled=True)
        return arrived.reshape(2, rows, columns)

    z_shape, g_shape = f32((2, EPOCHS) + fold), f32((2, pairs) + fold)
    tables = [
        pltpu.VMEM((2 * pairs + 1, 2) + fold, jnp.float32),
        pltpu.VMEM((EPOCHS + 1, 2) + fold, jnp.float32),
    ]
    small = [smem_spec()] * 3
    z, g, predicted = pl.pallas_call(
        invert_first_kernel,
        out_shape=(z_shape, g_shape, g_shape),
        in_specs=small + [vmem_spec()],
        out_specs=(vmem_spec(),) * 3,
        scratch_shapes=tables + [tables[1]],
        compiler_params=params(),
        name="invert_first",
    )(coef, seg, ends, spread(motion))
    motion = pl.pallas_call(
        again_kernel,
        out_shape=f32((2, rows, columns)),
        in_specs=[smem_spec()] + [vmem_spec()] * 3,
        out_specs=vmem_spec(),
        scratch_shapes=weight_scratch(steps, columns),
        compiler_params=params(),
        name="match_again",
    )(offsets, e, prior, collect(predicted))
    z, g = pl.pallas_call(
        invert_last_kernel,
        out_shape=(z_shape, g_shape),
        in_specs=small + [vmem_spec()] * 3,
        out_specs=(vmem_spec(),) * 2,
        scratch_shapes=tables,
        compiler_params=params(),
        name="invert_last",
    )(coef, seg, ends, spread(motion), z, g)
    return (z.reshape(2, EPOCHS, 1, pixels), motion[:, None])


def solution(mesh):
    placed = (
        P(("groups", "pairs"), "rows", None),
        P(("groups", "pairs"), "rows", None),
        P(None, ("groups", "pairs"), "rows", None),
        P(),
        P("groups", None),
        P("groups"),
    )
    return jax.shard_map(
        per_device,
        mesh=mesh,
        in_specs=placed,
        out_specs=(
            P(None, None, ("groups", "rows"), "pairs"),
            P(None, ("groups", "pairs"), "rows", None),
        ),
        check_vma=False,
    )
```

```python
import functools

import jax
import jax.numpy as jnp
from jax import lax
from jax.experimental import pallas as pl
from jax.experimental.pallas import tpu as pltpu
from jax.sharding import PartitionSpec as P

SEARCH = 4
RADIUS = 4
EPOCHS = 128
ITERS = 4
ROUNDS = 2

SOFTMIN_HEAT = 0.1
PRIOR_STRENGTH = 0.05
PENALTY = 4.0
SPARSITY = 0.4
VARIANCE_FLOOR = 0.05
HIGHEST = lax.Precision.HIGHEST

SIDE = 2 * SEARCH + 1
WINDOW = 2 * RADIUS + 1
MARGIN = SEARCH + RADIUS
SUB = 8
LANES = 128
AREA = 1.0 / float(WINDOW * WINDOW)
VMEM_BYTES = 40 * 1024 * 1024
BLOCK = 4


def vmem_spec():
    return pl.BlockSpec(memory_space=pltpu.VMEM)


def smem_spec():
    return pl.BlockSpec(memory_space=pltpu.SMEM)


def params(**more):
    return pltpu.CompilerParams(vmem_limit_bytes=VMEM_BYTES, **more)


def parts_of(values):
    high = values.astype(jnp.bfloat16)
    rest = values - high.astype(jnp.float32)
    middle = rest.astype(jnp.bfloat16)
    low = (rest - middle.astype(jnp.float32)).astype(jnp.bfloat16)
    return high, middle, low


def band_matrix(columns, shift):
    row = lax.broadcasted_iota(jnp.int32, (columns, columns), 0)
    col = lax.broadcasted_iota(jnp.int32, (columns, columns), 1)
    return (jnp.abs(row - col - shift) <= RADIUS).astype(jnp.float32).astype(jnp.bfloat16)


def column_box(values, band):
    high, middle, low = parts_of(values)
    mm = functools.partial(jnp.dot, preferred_element_type=jnp.float32)
    return mm(high, band) + (mm(middle, band) + mm(low, band))


def row_box(planes, count):
    result = []
    for base in range(0, count, SUB):
        mid = base + WINDOW - 2
        suffix = {mid: planes[mid]}
        for i in range(mid - 1, base - 1, -1):
            suffix[i] = planes[i] + suffix[i + 1]
        prefix = {mid + 1: planes[mid + 1]}
        for i in range(mid + 2, base + SUB - 1 + WINDOW):
            prefix[i] = prefix[i - 1] + planes[i]
        for i in range(base, base + SUB):
            result.append(suffix[i] + prefix[i + WINDOW - 1])
    return result


def inverse_root(values):
    guess = lax.rsqrt(values)
    return guess * (1.5 - 0.5 * values * guess * guess)


def split_lanes(values):
    return jnp.stack([values[:, i : i + LANES] for i in range(0, values.shape[1], LANES)])


def strided(ref, start, stride):
    rows = pl.ds(start, SUB, stride=stride)
    return jnp.concatenate([ref[i, rows, :] for i in range(ref.shape[0])], axis=-1)


def store_strided(ref, start, stride, values):
    rows = pl.ds(start, SUB, stride=stride)
    for i in range(ref.shape[0]):
        ref[i, rows, :] = values[:, i * LANES : (i + 1) * LANES]


def prepare(image_ref, f_ref, s_ref, mean_ref, inv_ref, mean1_ref, inv1_ref):
    rows = image_ref.shape[2] - 2 * MARGIN
    columns = image_ref.shape[1] * LANES
    steps = rows // SUB
    band = band_matrix(columns, 0)

    raw = [strided(image_ref.at[0], SEARCH + t, steps) for t in range(steps + 2 * RADIUS)]
    scaled = [x * AREA for x in raw]
    for t, x in enumerate(scaled):
        f_ref[t] = x
    sums = row_box(scaled, steps) + row_box([a * b for a, b in zip(raw, scaled)], steps)
    boxed = column_box(jnp.concatenate(sums, axis=0), band)
    mean1 = boxed[:rows]
    var1 = boxed[rows:] - mean1 * mean1
    mean1_ref[...] = mean1.reshape(steps, SUB, columns)
    inv1 = inverse_root(jnp.maximum(var1, VARIANCE_FLOOR)) * (1.0 / SOFTMIN_HEAT)
    inv1_ref[...] = inv1.reshape(steps, SUB, columns)

    reach = steps + 2 * MARGIN
    second = [strided(image_ref.at[1], t, steps) for t in range(reach)]
    wide = steps + 2 * SEARCH
    sums = row_box(second, wide) + row_box([x * x for x in second], wide)
    sums = parts_of(jnp.concatenate(sums, axis=0))
    stacked = jnp.concatenate(second, axis=0)
    lane = lax.broadcasted_iota(jnp.int32, stacked.shape, 1)
    half = wide * SUB
    for place in range(SIDE):
        shift = place - SEARCH
        moved = pltpu.roll(stacked, (-shift) % columns, 1) if shift else stacked
        inside = (lane + shift >= 0) & (lane + shift < columns)
        s_ref[place] = jnp.where(inside, moved, 0.0).reshape(reach, SUB, columns)
        shifted_band = band_matrix(columns, shift)
        mm = functools.partial(jnp.dot, preferred_element_type=jnp.float32)
        boxed = mm(sums[0], shifted_band) + (
            mm(sums[1], shifted_band) + mm(sums[2], shifted_band)
        )
        boxed = boxed * AREA
        mean = boxed[:half]
        var = boxed[half:] - mean * mean
        mean_ref[place] = mean.reshape(wide, SUB, columns)
        inv = inverse_root(jnp.maximum(var, VARIANCE_FLOOR))
        inv_ref[place] = inv.reshape(wide, SUB, columns)


def correlate(offsets_ref, f_ref, s_ref, mean_ref, inv_ref, mean1_ref, inv1_ref, e_ref):
    steps, _, columns = mean1_ref.shape
    rows = steps * SUB
    band = band_matrix(columns, 0)
    count = offsets_ref.shape[0]
    block = BLOCK if count % BLOCK == 0 else 1

    def body(number, carry):
        sums = []
        for i in range(block):
            k = number * block + i
            oy = offsets_ref[k, 0] + SEARCH
            ox = offsets_ref[k, 1] + SEARCH
            planes = [f_ref[t] * s_ref[ox, oy + t] for t in range(steps + 2 * RADIUS)]
            sums += row_box(planes, steps)
        boxed = column_box(jnp.concatenate(sums, axis=0), band)
        for i in range(block):
            k = number * block + i
            oy = offsets_ref[k, 0] + SEARCH
            ox = offsets_ref[k, 1] + SEARCH
            for t in range(steps):
                at = i * rows + t * SUB
                cov = boxed[at : at + SUB] - mean1_ref[t] * mean_ref[ox, oy + t]
                e_ref[k, t] = jnp.exp(cov * (inv1_ref[t] * inv_ref[ox, oy + t]))
        return carry

    lax.fori_loop(0, count // block, body, 0)


def prior_tables(prior_row, prior_col, a_ref, b_ref, lanes):
    steps = a_ref.shape[1]
    curve = 0.5 * (2.0 * PRIOR_STRENGTH / SOFTMIN_HEAT)
    for t in range(steps):
        for ref, prior in ((a_ref, prior_row(t)), (b_ref, prior_col(t))):
            near = jnp.clip(jnp.floor(prior + 0.5), -float(SEARCH), float(SEARCH))
            twice = near - 2.0 * prior
            for place in range(SIDE):
                i = float(place - SEARCH)
                ref[place, t, :, lanes] = jnp.exp(curve * ((near - i) * (twice + i)))


def match(offsets_ref, e_ref, a_ref, b_ref, lanes, together, store):
    count, steps = e_ref.shape[:2]
    for base in range(0, steps, together):
        here = pl.ds(base, together)
        zero = jnp.zeros((together, SUB, lanes.size), jnp.float32)

        def body(k, carry):
            total, rows, cols = carry
            oy = offsets_ref[k, 0]
            ox = offsets_ref[k, 1]
            table = a_ref[oy + SEARCH, here, :, lanes] * b_ref[ox + SEARCH, here, :, lanes]
            weight = e_ref[k, here, :, lanes] * table
            return (
                total + weight,
                rows + weight * oy.astype(jnp.float32),
                cols + weight * ox.astype(jnp.float32),
            )

        total, rows, cols = lax.fori_loop(0, count, body, (zero, zero, zero), unroll=8)
        for i in range(together):
            store(base + i, rows[i] / total[i], cols[i] / total[i])


def design_kernel(epochs_ref, slot_ref, coef_ref, seg_ref, ends_ref):
    pairs = slot_ref.shape[0]
    ends = 2 * pairs
    row_id = lax.broadcasted_iota(jnp.int32, (pairs, pairs), 0)
    col_id = lax.broadcasted_iota(jnp.int32, (pairs, pairs), 1)
    end_id = lax.broadcasted_iota(jnp.int32, (ends, pairs), 0)
    end_col = lax.broadcasted_iota(jnp.int32, (ends, pairs), 1)
    seg_id = lax.broadcasted_iota(jnp.int32, (ends, EPOCHS), 0)
    epoch = lax.broadcasted_iota(jnp.int32, (ends, EPOCHS), 1)

    def gather(j, state):
        first_r, after_r, first_c, after_c, mark, mark_e, first_e, after_e = state
        first = epochs_ref[slot_ref[j], 0]
        after = epochs_ref[slot_ref[j], 1]
        ends_ref[0, j] = first
        ends_ref[1, j] = after
        return (
            jnp.where(row_id == j, first, first_r),
            jnp.where(row_id == j, after, after_r),
            jnp.where(col_id == j, first, first_c),
            jnp.where(col_id == j, after, after_c),
            jnp.where(end_id == j, first, jnp.where(end_id == j + pairs, after, mark)),
            jnp.where(seg_id == j, first, jnp.where(seg_id == j + pairs, after, mark_e)),
            jnp.where(end_col == j, first, first_e),
            jnp.where(end_col == j, after, after_e),
        )

    square = jnp.zeros((pairs, pairs), jnp.int32)
    tall = jnp.zeros((ends, pairs), jnp.int32)
    state = (square, square, square, square, tall, jnp.zeros((ends, EPOCHS), jnp.int32), tall, tall)
    first_r, after_r, first_c, after_c, mark, mark_e, first_e, after_e = lax.fori_loop(
        0, pairs, gather, state
    )
    overlap = jnp.maximum(jnp.minimum(after_r, after_c) - jnp.maximum(first_r, first_c), 0)
    matrix = overlap.astype(jnp.float32) + jnp.where(row_id == col_id, PENALTY, 0.0)

    def eliminate(j, a):
        on_row = row_id == j
        on_col = col_id == j
        row = jnp.sum(jnp.where(on_row, a, 0.0), axis=0, keepdims=True)
        col = jnp.sum(jnp.where(on_col, a, 0.0), axis=1, keepdims=True)
        pivot = jnp.sum(jnp.where(col_id[:1] == j, row, 0.0), axis=1, keepdims=True)
        scale = 1.0 / pivot
        inner = a - col * (row * scale)
        return jnp.where(
            on_row,
            jnp.where(on_col, scale, row * scale),
            jnp.where(on_col, -col * scale, inner),
        )

    inverse = lax.fori_loop(0, pairs, eliminate, matrix)
    inside = ((mark >= first_e) & (mark < after_e)).astype(jnp.float32)
    coef = jnp.dot(inside, inverse, precision=HIGHEST, preferred_element_type=jnp.float32)
    wider = coef_ref.shape[1] - pairs
    if wider:
        coef = jnp.concatenate([coef, jnp.zeros((ends, wider), jnp.float32)], axis=1)
    coef_ref[...] = coef
    latest = jnp.max(jnp.where(mark_e <= epoch, mark_e, -1), axis=0, keepdims=True)
    which = jnp.max(jnp.where(mark_e == latest, seg_id, -1), axis=0, keepdims=True)
    seg_ref[...] = jnp.broadcast_to(jnp.where(latest < 0, ends, which), seg_ref.shape)


def design(pair_epochs, pair_slot):
    pairs = pair_slot.shape[0]
    return pl.pallas_call(
        design_kernel,
        out_shape=(
            jax.ShapeDtypeStruct((2 * pairs, pairs), jnp.float32),
            jax.ShapeDtypeStruct((1, EPOCHS), jnp.int32),
            jax.ShapeDtypeStruct((2, pairs), jnp.int32),
        ),
        in_specs=[smem_spec(), smem_spec()],
        out_specs=(vmem_spec(), vmem_spec(), smem_spec()),
        compiler_params=params(),
        name="design",
    )(pair_epochs, pair_slot)


def invert(coef_ref, seg_ref, ends_ref, pairs, d, begin, z, g, t_ref, cum_ref, predict):
    ends = 2 * pairs
    threshold = SPARSITY / PENALTY
    zero = jnp.zeros(t_ref.shape[1:], jnp.float32)
    t_ref[ends] = zero
    cum_ref[0] = zero
    if predict is not None:
        predict[1][0] = zero
    short = pairs <= 16

    for iteration in range(ITERS):
        start = begin is None and iteration == 0
        z_from, g_from = begin if begin and iteration == 0 else (z[0], g[0])
        last = iteration + 1 == ITERS
        summing = last and predict is not None

        def residual(p):
            return d(p) if start else d(p) - g_from(p)

        if short:
            gaps = [residual(p) for p in range(pairs)]
            for j in range(ends):
                value = coef_ref[j, 0] * gaps[0]
                for p in range(1, pairs):
                    value = value + coef_ref[j, p] * gaps[p]
                t_ref[j] = value
        else:

            def fill(j):
                t_ref[j] = lax.fori_loop(
                    0, pairs, lambda p, v: v + coef_ref[j, p] * residual(p), zero
                )

            pl.loop(0, ends)(fill)

        def epoch_step(e, carry):
            s = t_ref[seg_ref[0, e]]
            if not start:
                s = s + z_from(e)
            u = jnp.clip(s, -threshold, threshold)
            new = s - u
            z[1](e, new, last)
            if last and not summing:
                return carry
            run = carry[0] + (new - u)
            cum_ref[e + 1] = run
            if not summing:
                return (run,)
            run_z = carry[1] + new
            predict[1][e + 1] = run_z
            return (run, run_z)

        lax.fori_loop(0, EPOCHS, epoch_step, (zero, zero) if summing else (zero,), unroll=8)
        if last and not summing:
            return

        def collect(p):
            first, after = ends_ref[0, p], ends_ref[1, p]
            g[1](p, cum_ref[after] - cum_ref[first])
            if summing:
                predict[0](p, predict[1][after] - predict[1][first])

        if short:
            for p in range(pairs):
                collect(p)
        else:
            pl.loop(0, pairs)(collect)


def second_axis(ref):
    def store(i, value, last=False):
        ref[:, i] = value

    return (lambda i: ref[:, i]), store


def match_scratch(steps, columns):
    plane = (SUB, columns)
    extended = (2, columns // LANES, steps * SUB + 2 * MARGIN, LANES)
    return [
        pltpu.VMEM(extended, jnp.float32),
        pltpu.VMEM((steps + 2 * RADIUS,) + plane, jnp.float32),
        pltpu.VMEM((SIDE, steps + 2 * MARGIN) + plane, jnp.float32),
        pltpu.VMEM((SIDE, steps + 2 * SEARCH) + plane, jnp.float32),
        pltpu.VMEM((SIDE, steps + 2 * SEARCH) + plane, jnp.float32),
        pltpu.VMEM((steps,) + plane, jnp.float32),
        pltpu.VMEM((steps,) + plane, jnp.float32),
    ]


def weight_scratch(steps, columns):
    tables = [pltpu.VMEM((SIDE, steps, SUB, columns), jnp.float32)] * 2
    return tables + [pltpu.VMEM((2, columns // LANES, steps * SUB, LANES), jnp.float32)]


def match_on(offsets_ref, e_ref, prior_ref, back_ref, a_ref, b_ref, field_ref, motion_ref):
    steps = e_ref.shape[1]
    for component in range(2):
        values = prior_ref[component]
        if back_ref is not None:
            values = 0.5 * (values + back_ref[component])
        field_ref[component] = split_lanes(values)

    def prior(component):
        return lambda t: strided(field_ref.at[component], t, steps)

    def store(t, row, col):
        store_strided(field_ref.at[0], t, steps, row)
        store_strided(field_ref.at[1], t, steps, col)

    lanes = pl.ds(0, e_ref.shape[3])
    prior_tables(prior(0), prior(1), a_ref, b_ref, lanes)
    match(offsets_ref, e_ref, a_ref, b_ref, lanes, 2, store)
    for component in range(2):
        halves = [field_ref[component, i] for i in range(field_ref.shape[1])]
        motion_ref[component] = jnp.concatenate(halves, axis=-1)


def first_kernel(offsets_ref, images_ref, prior_ref, e_ref, motion_ref, *scratch):
    image_ref, *tables = scratch[:7]
    for i in range(2):
        image_ref[i] = split_lanes(images_ref[i])
    prepare(image_ref, *tables)
    correlate(offsets_ref, *tables, e_ref)
    match_on(offsets_ref, e_ref, prior_ref, None, *scratch[7:], motion_ref)


def again_kernel(offsets_ref, e_ref, prior_ref, back_ref, motion_ref, *scratch):
    match_on(offsets_ref, e_ref, prior_ref, back_ref, *scratch, motion_ref)


def invert_first_kernel(coef_ref, seg_ref, ends_ref, d_ref, z_ref, g_ref, gz_ref, t_ref, cum_ref, cumz_ref):
    z, g, d, gz = (second_axis(ref) for ref in (z_ref, g_ref, d_ref, gz_ref))
    tables = (coef_ref, seg_ref, ends_ref, d_ref.shape[1])
    invert(*tables, d[0], None, z, g, t_ref, cum_ref, (gz[1], cumz_ref))


def invert_last_kernel(coef_ref, seg_ref, ends_ref, d_ref, zin_ref, gin_ref, z_ref, g_ref, t_ref, cum_ref):
    z, g, d = (second_axis(ref) for ref in (z_ref, g_ref, d_ref))
    begin = (second_axis(zin_ref)[0], second_axis(gin_ref)[0])
    tables = (coef_ref, seg_ref, ends_ref, d_ref.shape[1])
    invert(*tables, d[0], begin, z, g, t_ref, cum_ref, None)


def fused_kernel(
    offsets_ref,
    epochs_ref,
    slot_ref,
    first_ref,
    second_ref,
    prior_ref,
    velocity_ref,
    motion_ref,
    image_ref,
    f_ref,
    s_ref,
    mean_ref,
    inv_ref,
    mean1_ref,
    inv1_ref,
    a_ref,
    b_ref,
    field_ref,
    e_ref,
    prior_split_ref,
    back_ref,
    edge_ref,
    halo_ref,
    d_ref,
    gz_ref,
    z_ref,
    g_ref,
    t_ref,
    cum_ref,
    cumz_ref,
    coef_vmem,
    seg_vmem,
    coef_ref,
    seg_ref,
    ends_ref,
    table_sem,
    halo_sem,
    send_sem,
    recv_sem,
):
    rows, columns = first_ref.shape
    steps = rows // SUB
    halves = columns // LANES
    pairs = slot_ref.shape[0]
    part = rows // pairs
    me = lax.axis_index("pairs")
    band = lax.axis_index("rows")
    mesh_id = pl.DeviceIdType.MESH

    barrier = pltpu.get_barrier_semaphore()
    peers = [lax.rem(me + i, pairs) for i in range(1, pairs)]
    pl.semaphore_signal(barrier, inc=1, device_id={"rows": 1 - band}, device_id_type=mesh_id)
    for peer in peers:
        pl.semaphore_signal(barrier, inc=1, device_id={"pairs": peer}, device_id_type=mesh_id)
    edge = pl.ds(pl.multiple_of((1 - band) * (rows - MARGIN), SUB), MARGIN)
    edge_ref[0] = first_ref[edge, :]
    edge_ref[1] = second_ref[edge, :]
    pl.semaphore_wait(barrier, pairs)
    halo = pltpu.make_async_remote_copy(
        src_ref=edge_ref,
        dst_ref=halo_ref,
        send_sem=halo_sem.at[0],
        recv_sem=halo_sem.at[1],
        device_id={"rows": 1 - band},
        device_id_type=mesh_id,
    )
    halo.start()

    design_kernel(epochs_ref, slot_ref, coef_vmem, seg_vmem, ends_ref)
    moves = [
        pltpu.make_async_copy(coef_vmem, coef_ref, table_sem.at[0]),
        pltpu.make_async_copy(seg_vmem, seg_ref, table_sem.at[1]),
    ]
    for move in moves:
        move.start()
    everywhere = pl.ds(0, columns)
    for component in range(2):
        prior_split_ref[component] = split_lanes(prior_ref[component])
    prior_tables(
        lambda t: strided(prior_split_ref.at[0], t, steps),
        lambda t: strided(prior_split_ref.at[1], t, steps),
        a_ref,
        b_ref,
        everywhere,
    )
    for i, ref in enumerate((first_ref, second_ref)):
        image_ref[i, :, MARGIN : MARGIN + rows, :] = split_lanes(ref[...])
    halo.wait()
    for i in range(2):
        arrived = split_lanes(halo_ref[i])
        image_ref[i, :, :MARGIN, :] = jnp.where(band == 1, arrived, 0.0)
        image_ref[i, :, MARGIN + rows :, :] = jnp.where(band == 0, arrived, 0.0)
    for move in moves:
        move.wait()
    prepare(image_ref, f_ref, s_ref, mean_ref, inv_ref, mean1_ref, inv1_ref)
    correlate(offsets_ref, f_ref, s_ref, mean_ref, inv_ref, mean1_ref, inv1_ref, e_ref)

    def block(index):
        return pl.ds(pl.multiple_of(index * part, SUB), part)

    def push(phase, half, source, target):
        copies = []
        for i, peer in enumerate(peers):
            copy = pltpu.make_async_remote_copy(
                src_ref=source(peer),
                dst_ref=target(me),
                send_sem=send_sem.at[phase, half, i],
                recv_sem=recv_sem.at[phase, half, i],
                device_id={"pairs": peer},
                device_id_type=mesh_id,
            )
            copy.start()
            copies.append(copy)
        target(me)[...] = source(me)[...]
        return copies

    def finish(copies):
        for copy in copies:
            copy.wait()

    def match_half(phase, half):
        lanes = pl.ds(half * LANES, LANES)

        def store(t, row, col):
            field_ref[0, half, pl.ds(t, SUB, stride=steps), :] = row
            field_ref[1, half, pl.ds(t, SUB, stride=steps), :] = col

        match(offsets_ref, e_ref, a_ref, b_ref, lanes, 4 if steps % 4 == 0 else 1, store)
        return push(
            phase,
            half,
            lambda q: field_ref.at[:, half, block(q), :],
            lambda q: d_ref.at[phase // 2, half, q],
        )

    def invert_half(phase, half):
        def store_z(e, value, last):
            if phase and last:
                for component in range(2):
                    place = pl.ds(half, part, stride=halves)
                    velocity_ref[component, e, place, :] = value[component]
            else:
                z_ref[half, e] = value

        def store_g(p, value):
            g_ref[half, p] = value

        def store_gz(p, value):
            gz_ref[half, p] = value

        z = ((lambda e: z_ref[half, e]), store_z)
        g = ((lambda p: g_ref[half, p]), store_g)
        invert(
            coef_ref,
            seg_ref,
            ends_ref,
            pairs,
            lambda p: d_ref[phase // 2, half, p],
            (z[0], g[0]) if phase else None,
            z,
            g,
            t_ref,
            cum_ref,
            None if phase else (store_gz, cumz_ref),
        )

    sent = [match_half(0, half) for half in range(halves)]
    returned = []
    for half in range(halves):
        finish(sent[half])
        invert_half(0, half)
        returned.append(
            push(
                1,
                half,
                lambda q: gz_ref.at[half, q],
                lambda q: back_ref.at[:, half, block(q), :],
            )
        )
    sent = []
    for half in range(halves):
        finish(returned[half])

        def prior(component):
            def at(t):
                place = pl.ds(t, SUB, stride=steps)
                given = prior_split_ref[component, half, place, :]
                return 0.5 * (given + back_ref[component, half, place, :])

            return at

        prior_tables(prior(0), prior(1), a_ref, b_ref, pl.ds(half * LANES, LANES))
        sent.append(match_half(2, half))
    for component in range(2):
        pieces = [field_ref[component, half] for half in range(halves)]
        motion_ref[component] = jnp.concatenate(pieces, axis=-1)
    for half in range(halves):
        finish(sent[half])
        invert_half(2, half)


def fused(first_image, second_image, prior, offsets, pair_epochs, pair_slot):
    rows, columns = first_image.shape
    steps, halves = rows // SUB, columns // LANES
    pairs = pair_slot.shape[0]
    part = rows // pairs
    f32 = jnp.float32
    plane = (2, part, LANES)
    split = (2, halves, rows, LANES)
    return pl.pallas_call(
        fused_kernel,
        out_shape=(
            jax.ShapeDtypeStruct((2, EPOCHS, part * halves, LANES), f32),
            jax.ShapeDtypeStruct((2, rows, columns), f32),
        ),
        in_specs=[smem_spec()] * 3 + [vmem_spec()] * 3,
        out_specs=(vmem_spec(), vmem_spec()),
        scratch_shapes=match_scratch(steps, columns)
        + weight_scratch(steps, columns)
        + [
            pltpu.VMEM((offsets.shape[0], steps, SUB, columns), f32),
            pltpu.VMEM(split, f32),
            pltpu.VMEM(split, f32),
            pltpu.VMEM((2, MARGIN, columns), f32),
            pltpu.VMEM((2, MARGIN, columns), f32),
            pltpu.VMEM((ROUNDS, halves, pairs) + plane, f32),
            pltpu.VMEM((halves, pairs) + plane, f32),
            pltpu.VMEM((halves, EPOCHS) + plane, f32),
            pltpu.VMEM((halves, pairs) + plane, f32),
            pltpu.VMEM((2 * pairs + 1,) + plane, f32),
            pltpu.VMEM((EPOCHS + 1,) + plane, f32),
            pltpu.VMEM((EPOCHS + 1,) + plane, f32),
            pltpu.VMEM((2 * pairs, LANES), f32),
            pltpu.VMEM((SUB, EPOCHS), jnp.int32),
            pltpu.SMEM((2 * pairs, LANES), f32),
            pltpu.SMEM((SUB, EPOCHS), jnp.int32),
            pltpu.SMEM((2, pairs), jnp.int32),
            pltpu.SemaphoreType.DMA((2,)),
            pltpu.SemaphoreType.DMA((2,)),
            pltpu.SemaphoreType.DMA((3, halves, pairs)),
            pltpu.SemaphoreType.DMA((3, halves, pairs)),
        ],
        compiler_params=params(collective_id=0, has_side_effects=True),
        name="track",
    )(offsets, pair_epochs, pair_slot, first_image, second_image, prior)


def with_halo(cells, axis, dim, width):
    count = lax.axis_size(axis)
    head = lax.slice_in_dim(cells, 0, width, axis=dim)
    tail = lax.slice_in_dim(cells, cells.shape[dim] - width, cells.shape[dim], axis=dim)
    down = lax.ppermute(tail, axis, [(i, i + 1) for i in range(count - 1)])
    up = lax.ppermute(head, axis, [(i + 1, i) for i in range(count - 1)])
    return jnp.concatenate([down, cells, up], axis=dim)


def per_device(first_image, second_image, prior_motion, offsets, pair_epochs, pair_slot):
    rows, columns = first_image.shape[1:]
    steps = rows // SUB
    pairs = lax.axis_size("pairs")
    pixels = rows * columns // pairs
    fold = (pixels // LANES, LANES) if pixels % LANES == 0 else (1, pixels)
    f32 = functools.partial(jax.ShapeDtypeStruct, dtype=jnp.float32)
    prior = prior_motion[:, 0]
    whole_tiles = rows % (SUB * pairs) == 0 and columns % LANES == 0 and pairs <= LANES
    if whole_tiles and lax.axis_size("rows") == 2:
        velocity, motion = fused(
            first_image[0], second_image[0], prior, offsets, pair_epochs, pair_slot
        )
        return (velocity.reshape(2, EPOCHS, 1, pixels), motion[:, None])
    coef, seg, ends = design(pair_epochs, pair_slot)
    images = with_halo(jnp.concatenate((first_image, second_image), axis=0), "rows", 1, MARGIN)
    e, motion = pl.pallas_call(
        first_kernel,
        out_shape=(f32((offsets.shape[0], steps, SUB, columns)), f32((2, rows, columns))),
        in_specs=[smem_spec(), vmem_spec(), vmem_spec()],
        out_specs=(vmem_spec(), vmem_spec()),
        scratch_shapes=match_scratch(steps, columns) + weight_scratch(steps, columns),
        compiler_params=params(),
        name="correlate",
    )(offsets, images, prior)

    def spread(field):
        outgoing = field.reshape(2, 1, pairs, pixels)
        arrived = lax.all_to_all(outgoing, "pairs", split_axis=2, concat_axis=1, tiled=True)
        return arrived.reshape((2, pairs) + fold)

    def collect(field):
        outgoing = field.reshape(2, pairs, 1, pixels)
        arrived = lax.all_to_all(outgoing, "pairs", split_axis=1, concat_axis=2, tiled=True)
        return arrived.reshape(2, rows, columns)

    z_shape, g_shape = f32((2, EPOCHS) + fold), f32((2, pairs) + fold)
    tables = [
        pltpu.VMEM((2 * pairs + 1, 2) + fold, jnp.float32),
        pltpu.VMEM((EPOCHS + 1, 2) + fold, jnp.float32),
    ]
    small = [smem_spec()] * 3
    z, g, predicted = pl.pallas_call(
        invert_first_kernel,
        out_shape=(z_shape, g_shape, g_shape),
        in_specs=small + [vmem_spec()],
        out_specs=(vmem_spec(),) * 3,
        scratch_shapes=tables + [tables[1]],
        compiler_params=params(),
        name="invert_first",
    )(coef, seg, ends, spread(motion))
    motion = pl.pallas_call(
        again_kernel,
        out_shape=f32((2, rows, columns)),
        in_specs=[smem_spec()] + [vmem_spec()] * 3,
        out_specs=vmem_spec(),
        scratch_shapes=weight_scratch(steps, columns),
        compiler_params=params(),
        name="match_again",
    )(offsets, e, prior, collect(predicted))
    z, g = pl.pallas_call(
        invert_last_kernel,
        out_shape=(z_shape, g_shape),
        in_specs=small + [vmem_spec()] * 3,
        out_specs=(vmem_spec(),) * 2,
        scratch_shapes=tables,
        compiler_params=params(),
        name="invert_last",
    )(coef, seg, ends, spread(motion), z, g)
    return (z.reshape(2, EPOCHS, 1, pixels), motion[:, None])


def solution(mesh):
    placed = (
        P(("groups", "pairs"), "rows", None),
        P(("groups", "pairs"), "rows", None),
        P(None, ("groups", "pairs"), "rows", None),
        P(),
        P("groups", None),
        P("groups"),
    )
    return jax.shard_map(
        per_device,
        mesh=mesh,
        in_specs=placed,
        out_specs=(
            P(None, None, ("groups", "rows"), "pairs"),
            P(None, ("groups", "pairs"), "rows", None),
        ),
        check_vma=False,
    )
```

```python
import functools

import jax
import jax.numpy as jnp
from jax import lax
from jax.experimental import pallas as pl
from jax.experimental.pallas import tpu as pltpu
from jax.sharding import PartitionSpec as P

SEARCH = 4
RADIUS = 4
EPOCHS = 128
ITERS = 4
ROUNDS = 2

SOFTMIN_HEAT = 0.1
PRIOR_STRENGTH = 0.05
PENALTY = 4.0
SPARSITY = 0.4
VARIANCE_FLOOR = 0.05
HIGHEST = lax.Precision.HIGHEST

SIDE = 2 * SEARCH + 1
WINDOW = 2 * RADIUS + 1
MARGIN = SEARCH + RADIUS
SUB = 8
LANES = 128
AREA = 1.0 / float(WINDOW * WINDOW)
VMEM_BYTES = 40 * 1024 * 1024
BLOCK = 4


def vmem_spec():
    return pl.BlockSpec(memory_space=pltpu.VMEM)


def smem_spec():
    return pl.BlockSpec(memory_space=pltpu.SMEM)


def params(**more):
    return pltpu.CompilerParams(vmem_limit_bytes=VMEM_BYTES, **more)


def parts_of(values):
    high = values.astype(jnp.bfloat16)
    rest = values - high.astype(jnp.float32)
    middle = rest.astype(jnp.bfloat16)
    low = (rest - middle.astype(jnp.float32)).astype(jnp.bfloat16)
    return high, middle, low


def band_matrix(columns, shift):
    row = lax.broadcasted_iota(jnp.int32, (columns, columns), 0)
    col = lax.broadcasted_iota(jnp.int32, (columns, columns), 1)
    return (jnp.abs(row - col - shift) <= RADIUS).astype(jnp.float32).astype(jnp.bfloat16)


def column_box(values, band):
    high, middle, low = parts_of(values)
    mm = functools.partial(jnp.dot, preferred_element_type=jnp.float32)
    return mm(high, band) + (mm(middle, band) + mm(low, band))


def row_box(planes, count):
    result = []
    for base in range(0, count, SUB):
        mid = base + WINDOW - 2
        suffix = {mid: planes[mid]}
        for i in range(mid - 1, base - 1, -1):
            suffix[i] = planes[i] + suffix[i + 1]
        prefix = {mid + 1: planes[mid + 1]}
        for i in range(mid + 2, base + SUB - 1 + WINDOW):
            prefix[i] = prefix[i - 1] + planes[i]
        for i in range(base, base + SUB):
            result.append(suffix[i] + prefix[i + WINDOW - 1])
    return result


def inverse_root(values):
    guess = lax.rsqrt(values)
    return guess * (1.5 - 0.5 * values * guess * guess)


def split_lanes(values):
    return jnp.stack([values[:, i : i + LANES] for i in range(0, values.shape[1], LANES)])


def strided(ref, start, stride):
    rows = pl.ds(start, SUB, stride=stride)
    return jnp.concatenate([ref[i, rows, :] for i in range(ref.shape[0])], axis=-1)


def store_strided(ref, start, stride, values):
    rows = pl.ds(start, SUB, stride=stride)
    for i in range(ref.shape[0]):
        ref[i, rows, :] = values[:, i * LANES : (i + 1) * LANES]


def prepare(image_ref, f_ref, s_ref, mean_ref, inv_ref, mean1_ref, inv1_ref):
    rows = image_ref.shape[2] - 2 * MARGIN
    columns = image_ref.shape[1] * LANES
    steps = rows // SUB
    band = band_matrix(columns, 0)

    raw = [strided(image_ref.at[0], SEARCH + t, steps) for t in range(steps + 2 * RADIUS)]
    scaled = [x * AREA for x in raw]
    for t, x in enumerate(scaled):
        f_ref[t] = x
    sums = row_box(scaled, steps) + row_box([a * b for a, b in zip(raw, scaled)], steps)
    boxed = column_box(jnp.concatenate(sums, axis=0), band)
    mean1 = boxed[:rows]
    var1 = boxed[rows:] - mean1 * mean1
    mean1_ref[...] = mean1.reshape(steps, SUB, columns)
    inv1 = inverse_root(jnp.maximum(var1, VARIANCE_FLOOR)) * (1.0 / SOFTMIN_HEAT)
    inv1_ref[...] = inv1.reshape(steps, SUB, columns)

    reach = steps + 2 * MARGIN
    second = [strided(image_ref.at[1], t, steps) for t in range(reach)]
    wide = steps + 2 * SEARCH
    sums = row_box(second, wide) + row_box([x * x for x in second], wide)
    sums = parts_of(jnp.concatenate(sums, axis=0))
    stacked = jnp.concatenate(second, axis=0)
    lane = lax.broadcasted_iota(jnp.int32, stacked.shape, 1)
    half = wide * SUB
    for place in range(SIDE):
        shift = place - SEARCH
        moved = pltpu.roll(stacked, (-shift) % columns, 1) if shift else stacked
        inside = (lane + shift >= 0) & (lane + shift < columns)
        s_ref[place] = jnp.where(inside, moved, 0.0).reshape(reach, SUB, columns)
        shifted_band = band_matrix(columns, shift)
        mm = functools.partial(jnp.dot, preferred_element_type=jnp.float32)
        boxed = mm(sums[0], shifted_band) + (
            mm(sums[1], shifted_band) + mm(sums[2], shifted_band)
        )
        boxed = boxed * AREA
        mean = boxed[:half]
        var = boxed[half:] - mean * mean
        mean_ref[place] = mean.reshape(wide, SUB, columns)
        inv = inverse_root(jnp.maximum(var, VARIANCE_FLOOR))
        inv_ref[place] = inv.reshape(wide, SUB, columns)


def correlate(shift, count, f_ref, s_ref, mean_ref, inv_ref, mean1_ref, inv1_ref, e_ref):
    steps, _, columns = mean1_ref.shape
    rows = steps * SUB
    band = band_matrix(columns, 0)
    block = BLOCK if count % BLOCK == 0 else 1

    def body(number, carry):
        sums = []
        for i in range(block):
            k = number * block + i
            oy, ox = shift(k)
            planes = [f_ref[t] * s_ref[ox, oy + t] for t in range(steps + 2 * RADIUS)]
            sums += row_box(planes, steps)
        boxed = column_box(jnp.concatenate(sums, axis=0), band)
        for i in range(block):
            k = number * block + i
            oy, ox = shift(k)
            for t in range(steps):
                at = i * rows + t * SUB
                cov = boxed[at : at + SUB] - mean1_ref[t] * mean_ref[ox, oy + t]
                e_ref[k, t] = jnp.exp(cov * (inv1_ref[t] * inv_ref[ox, oy + t]))
        return carry

    lax.fori_loop(0, count // block, body, 0)


def prior_tables(prior_row, prior_col, a_ref, b_ref, lanes):
    steps = a_ref.shape[1]
    curve = 0.5 * (2.0 * PRIOR_STRENGTH / SOFTMIN_HEAT)
    for t in range(steps):
        for ref, prior in ((a_ref, prior_row(t)), (b_ref, prior_col(t))):
            near = jnp.clip(jnp.floor(prior + 0.5), -float(SEARCH), float(SEARCH))
            twice = near - 2.0 * prior
            for place in range(SIDE):
                i = float(place - SEARCH)
                ref[place, t, :, lanes] = jnp.exp(curve * ((near - i) * (twice + i)))


def match(offsets_ref, e_ref, a_ref, b_ref, lanes, together, store):
    count, steps = e_ref.shape[:2]
    for base in range(0, steps, together):
        here = pl.ds(base, together)
        zero = jnp.zeros((together, SUB, lanes.size), jnp.float32)

        def body(k, carry):
            total, rows, cols = carry
            oy = offsets_ref[k, 0]
            ox = offsets_ref[k, 1]
            table = a_ref[oy + SEARCH, here, :, lanes] * b_ref[ox + SEARCH, here, :, lanes]
            weight = e_ref[k, here, :, lanes] * table
            return (
                total + weight,
                rows + weight * oy.astype(jnp.float32),
                cols + weight * ox.astype(jnp.float32),
            )

        total, rows, cols = lax.fori_loop(0, count, body, (zero, zero, zero), unroll=8)
        for i in range(together):
            store(base + i, rows[i] / total[i], cols[i] / total[i])


def match_cells(cell, e_ref, a_ref, b_ref, lanes, together, store):
    steps = e_ref.shape[1]
    for base in range(0, steps, together):
        here = pl.ds(base, together)
        zero = jnp.zeros((together, SUB, lanes.size), jnp.float32)
        table = [b_ref[j, here, :, lanes] for j in range(SIDE)]
        moment = [x * float(j - SEARCH) for j, x in enumerate(table)]

        def body(i, carry):
            total, rows, cols = carry
            first, second = zero, zero
            for j in range(SIDE):
                e = e_ref[cell(i * SIDE + j), here, :, lanes]
                first = first + e * table[j]
                if j != SEARCH:
                    second = second + e * moment[j]
            a = a_ref[i, here, :, lanes]
            weight = a * first
            shift = lax.convert_element_type(i - SEARCH, jnp.float32)
            return total + weight, rows + weight * shift, cols + a * second

        total, rows, cols = lax.fori_loop(0, SIDE, body, (zero, zero, zero), unroll=True)
        for i in range(together):
            store(base + i, rows[i] / total[i], cols[i] / total[i])


def design_kernel(epochs_ref, slot_ref, coef_ref, seg_ref, ends_ref, weigh=False):
    pairs = slot_ref.shape[0]
    ends = 2 * pairs
    row_id = lax.broadcasted_iota(jnp.int32, (pairs, pairs), 0)
    col_id = lax.broadcasted_iota(jnp.int32, (pairs, pairs), 1)
    end_id = lax.broadcasted_iota(jnp.int32, (ends, pairs), 0)
    end_col = lax.broadcasted_iota(jnp.int32, (ends, pairs), 1)
    seg_id = lax.broadcasted_iota(jnp.int32, (ends, EPOCHS), 0)
    epoch = lax.broadcasted_iota(jnp.int32, (ends, EPOCHS), 1)

    def gather(j, state):
        first_r, after_r, first_c, after_c, mark, mark_e, first_e, after_e = state
        first = epochs_ref[0, slot_ref[j]]
        after = epochs_ref[1, slot_ref[j]]
        if ends_ref is not None:
            ends_ref[0, j] = first
            ends_ref[1, j] = after
        return (
            jnp.where(row_id == j, first, first_r),
            jnp.where(row_id == j, after, after_r),
            jnp.where(col_id == j, first, first_c),
            jnp.where(col_id == j, after, after_c),
            jnp.where(end_id == j, first, jnp.where(end_id == j + pairs, after, mark)),
            jnp.where(seg_id == j, first, jnp.where(seg_id == j + pairs, after, mark_e)),
            jnp.where(end_col == j, first, first_e),
            jnp.where(end_col == j, after, after_e),
        )

    square = jnp.zeros((pairs, pairs), jnp.int32)
    tall = jnp.zeros((ends, pairs), jnp.int32)
    state = (square, square, square, square, tall, jnp.zeros((ends, EPOCHS), jnp.int32), tall, tall)
    first_r, after_r, first_c, after_c, mark, mark_e, first_e, after_e = lax.fori_loop(
        0, pairs, gather, state
    )
    overlap = jnp.maximum(jnp.minimum(after_r, after_c) - jnp.maximum(first_r, first_c), 0)
    matrix = overlap.astype(jnp.float32) + jnp.where(row_id == col_id, PENALTY, 0.0)

    def eliminate(j, a):
        on_row = row_id == j
        on_col = col_id == j
        row = jnp.sum(jnp.where(on_row, a, 0.0), axis=0, keepdims=True)
        col = jnp.sum(jnp.where(on_col, a, 0.0), axis=1, keepdims=True)
        pivot = jnp.sum(jnp.where(col_id[:1] == j, row, 0.0), axis=1, keepdims=True)
        scale = 1.0 / pivot
        inner = a - col * (row * scale)
        return jnp.where(
            on_row,
            jnp.where(on_col, scale, row * scale),
            jnp.where(on_col, -col * scale, inner),
        )

    inverse = lax.fori_loop(0, pairs, eliminate, matrix)
    inside = ((mark >= first_e) & (mark < after_e)).astype(jnp.float32)
    latest = jnp.max(jnp.where(mark_e <= epoch, mark_e, -1), axis=0, keepdims=True)
    which = jnp.max(jnp.where(mark_e == latest, seg_id, -1), axis=0, keepdims=True)
    which = jnp.where(latest < 0, ends, which)
    seg_ref[0:1] = which
    coef = jnp.dot(inside, inverse, precision=HIGHEST, preferred_element_type=jnp.float32)
    if weigh:
        long = jnp.sum((which == seg_id).astype(jnp.float32), axis=1, keepdims=True)
        blank = jnp.zeros((ends, coef_ref.shape[1] - ends), jnp.float32)
        coef = jnp.concatenate([coef, inside * long, blank], axis=1)
    coef_ref[...] = coef


def design(pair_epochs, pair_slot):
    pairs = pair_slot.shape[0]
    return pl.pallas_call(
        design_kernel,
        out_shape=(
            jax.ShapeDtypeStruct((2 * pairs, pairs), jnp.float32),
            jax.ShapeDtypeStruct((1, EPOCHS), jnp.int32),
            jax.ShapeDtypeStruct((2, pairs), jnp.int32),
        ),
        in_specs=[smem_spec(), smem_spec()],
        out_specs=(vmem_spec(), vmem_spec(), smem_spec()),
        compiler_params=params(),
        name="design",
    )(pair_epochs.T, pair_slot)


def invert(coef_ref, seg_ref, ends_ref, pairs, d, begin, z, g, t_ref, cum_ref, predict):
    ends = 2 * pairs
    threshold = SPARSITY / PENALTY
    zero = jnp.zeros(t_ref.shape[1:], jnp.float32)
    t_ref[ends] = zero
    cum_ref[0] = zero
    if predict is not None:
        predict[1][0] = zero
    short = pairs <= 16

    for iteration in range(ITERS):
        start = begin is None and iteration == 0
        z_from, g_from = begin if begin and iteration == 0 else (z[0], g[0])
        last = iteration + 1 == ITERS
        summing = last and predict is not None

        def residual(p):
            return d(p) if start else d(p) - g_from(p)

        if short:
            gaps = [residual(p) for p in range(pairs)]
            for j in range(ends):
                value = coef_ref[j, 0] * gaps[0]
                for p in range(1, pairs):
                    value = value + coef_ref[j, p] * gaps[p]
                t_ref[j] = value
        else:

            def fill(j):
                t_ref[j] = lax.fori_loop(
                    0, pairs, lambda p, v: v + coef_ref[j, p] * residual(p), zero
                )

            pl.loop(0, ends)(fill)

        def epoch_step(e, carry):
            s = t_ref[seg_ref[0, e]]
            if not start:
                s = s + z_from(e)
            u = jnp.clip(s, -threshold, threshold)
            new = s - u
            z[1](e, new, last)
            if last and not summing:
                return carry
            run = carry[0] + (new - u)
            cum_ref[e + 1] = run
            if not summing:
                return (run,)
            run_z = carry[1] + new
            predict[1][e + 1] = run_z
            return (run, run_z)

        lax.fori_loop(0, EPOCHS, epoch_step, (zero, zero) if summing else (zero,), unroll=8)
        if last and not summing:
            return

        def collect(p):
            first, after = ends_ref[0, p], ends_ref[1, p]
            g[1](p, cum_ref[after] - cum_ref[first])
            if summing:
                predict[0](p, predict[1][after] - predict[1][first])

        if short:
            for p in range(pairs):
                collect(p)
        else:
            pl.loop(0, pairs)(collect)


def invert_segments(coef_ref, pairs, d, z_ref, g_ref, fresh):
    ends = 2 * pairs
    threshold = SPARSITY / PENALTY
    zero = jnp.zeros(z_ref.shape[1:], jnp.float32)
    if fresh:
        for j in range(ends + 1):
            z_ref[j] = zero
    seen = [d(p) for p in range(pairs)]

    def weigh(j, value, sums):
        return tuple(g + coef_ref[j, pairs + p] * value for p, g in enumerate(sums))

    def step(iteration, held):
        gaps = [a - b for a, b in zip(seen, held)]
        sums = (zero,) * pairs
        for j in range(ends):
            terms = [coef_ref[j, p] * gap for p, gap in enumerate(gaps)]
            while len(terms) > 1:
                terms = [sum(terms[i : i + 2][1:], terms[i]) for i in range(0, len(terms), 2)]
            s = z_ref[j] + terms[0]
            u = jnp.clip(s, -threshold, threshold)
            z = s - u
            z_ref[j] = z
            sums = weigh(j, z - u, sums)
        return sums

    held = (zero,) * pairs if fresh else tuple(g_ref[p] for p in range(pairs))
    held = lax.fori_loop(0, ITERS, step, held)
    if not fresh:
        return None
    for p in range(pairs):
        g_ref[p] = held[p]
    sums = (zero,) * pairs
    for j in range(ends):
        sums = weigh(j, z_ref[j], sums)
    return sums


def second_axis(ref):
    def store(i, value, last=False):
        ref[:, i] = value

    return (lambda i: ref[:, i]), store


def match_scratch(steps, columns):
    plane = (SUB, columns)
    extended = (2, columns // LANES, steps * SUB + 2 * MARGIN, LANES)
    return [
        pltpu.VMEM(extended, jnp.float32),
        pltpu.VMEM((steps + 2 * RADIUS,) + plane, jnp.float32),
        pltpu.VMEM((SIDE, steps + 2 * MARGIN) + plane, jnp.float32),
        pltpu.VMEM((SIDE, steps + 2 * SEARCH) + plane, jnp.float32),
        pltpu.VMEM((SIDE, steps + 2 * SEARCH) + plane, jnp.float32),
        pltpu.VMEM((steps,) + plane, jnp.float32),
        pltpu.VMEM((steps,) + plane, jnp.float32),
    ]


def weight_scratch(steps, columns):
    tables = [pltpu.VMEM((SIDE, steps, SUB, columns), jnp.float32)] * 2
    return tables + [pltpu.VMEM((2, columns // LANES, steps * SUB, LANES), jnp.float32)]


def match_on(offsets_ref, e_ref, prior_ref, back_ref, a_ref, b_ref, field_ref, motion_ref):
    steps = e_ref.shape[1]
    for component in range(2):
        values = prior_ref[component]
        if back_ref is not None:
            values = 0.5 * (values + back_ref[component])
        field_ref[component] = split_lanes(values)

    def prior(component):
        return lambda t: strided(field_ref.at[component], t, steps)

    def store(t, row, col):
        store_strided(field_ref.at[0], t, steps, row)
        store_strided(field_ref.at[1], t, steps, col)

    lanes = pl.ds(0, e_ref.shape[3])
    prior_tables(prior(0), prior(1), a_ref, b_ref, lanes)
    match(offsets_ref, e_ref, a_ref, b_ref, lanes, 2, store)
    for component in range(2):
        halves = [field_ref[component, i] for i in range(field_ref.shape[1])]
        motion_ref[component] = jnp.concatenate(halves, axis=-1)


def first_kernel(offsets_ref, images_ref, prior_ref, e_ref, motion_ref, *scratch):
    image_ref, *tables = scratch[:7]
    for i in range(2):
        image_ref[i] = split_lanes(images_ref[i])
    prepare(image_ref, *tables)
    shift = lambda k: (offsets_ref[k, 0] + SEARCH, offsets_ref[k, 1] + SEARCH)
    correlate(shift, offsets_ref.shape[0], *tables, e_ref)
    match_on(offsets_ref, e_ref, prior_ref, None, *scratch[7:], motion_ref)


def again_kernel(offsets_ref, e_ref, prior_ref, back_ref, motion_ref, *scratch):
    match_on(offsets_ref, e_ref, prior_ref, back_ref, *scratch, motion_ref)


def invert_first_kernel(coef_ref, seg_ref, ends_ref, d_ref, z_ref, g_ref, gz_ref, t_ref, cum_ref, cumz_ref):
    z, g, d, gz = (second_axis(ref) for ref in (z_ref, g_ref, d_ref, gz_ref))
    tables = (coef_ref, seg_ref, ends_ref, d_ref.shape[1])
    invert(*tables, d[0], None, z, g, t_ref, cum_ref, (gz[1], cumz_ref))


def invert_last_kernel(coef_ref, seg_ref, ends_ref, d_ref, zin_ref, gin_ref, z_ref, g_ref, t_ref, cum_ref):
    z, g, d = (second_axis(ref) for ref in (z_ref, g_ref, d_ref))
    begin = (second_axis(zin_ref)[0], second_axis(gin_ref)[0])
    tables = (coef_ref, seg_ref, ends_ref, d_ref.shape[1])
    invert(*tables, d[0], begin, z, g, t_ref, cum_ref, None)


def fused_kernel(
    offsets_hbm,
    epochs_hbm,
    slot_hbm,
    first_hbm,
    second_hbm,
    prior_hbm,
    velocity_ref,
    motion_ref,
    image_ref,
    f_ref,
    s_ref,
    mean_ref,
    inv_ref,
    mean1_ref,
    inv1_ref,
    a_ref,
    b_ref,
    field_ref,
    e_ref,
    prior_ref,
    back_ref,
    d_ref,
    gz_ref,
    z_ref,
    g_ref,
    coef_vmem,
    index_vmem,
    coef_ref,
    index_ref,
    offsets_ref,
    epochs_ref,
    slot_ref,
    load_sem,
    table_sem,
    halo_sem,
    send_sem,
    recv_sem,
):
    rows, columns = first_hbm.shape
    steps = rows // SUB
    halves = columns // LANES
    pairs = slot_ref.shape[0]
    part = rows // pairs
    count = offsets_ref.shape[1]
    me = lax.axis_index("pairs")
    band = lax.axis_index("rows")
    mesh_id = pl.DeviceIdType.MESH

    barrier = pltpu.get_barrier_semaphore()
    peers = [lax.rem(me + i, pairs) for i in range(1, pairs)]
    pl.semaphore_signal(barrier, inc=1, device_id={"rows": 1 - band}, device_id_type=mesh_id)
    for peer in peers:
        pl.semaphore_signal(barrier, inc=1, device_id={"pairs": peer}, device_id_type=mesh_id)

    moves = [(epochs_hbm, epochs_ref), (slot_hbm, slot_ref), (offsets_hbm, offsets_ref)]
    for half in range(halves):
        lanes = pl.ds(half * LANES, LANES)
        inner = pl.ds(MARGIN, rows)
        moves += [
            (prior_hbm.at[0, :, lanes], prior_ref.at[0, half]),
            (prior_hbm.at[1, :, lanes], prior_ref.at[1, half]),
            (first_hbm.at[:, lanes], image_ref.at[0, half, inner]),
            (second_hbm.at[:, lanes], image_ref.at[1, half, inner]),
        ]
    loads = [
        pltpu.make_async_copy(source, target, load_sem.at[i])
        for i, (source, target) in enumerate(moves)
    ]
    for load in loads:
        load.start()
    outer = pl.ds(pl.multiple_of(band * (rows + MARGIN), SUB), MARGIN)
    edge = pl.ds(pl.multiple_of((1 - band) * (rows - MARGIN), SUB), MARGIN)
    image_ref[:, :, outer, :] = jnp.zeros((2, halves, MARGIN, LANES), jnp.float32)
    pl.semaphore_wait(barrier, pairs)
    halos = []
    for i, source in enumerate((first_hbm, second_hbm)):
        for half in range(halves):
            halo = pltpu.make_async_remote_copy(
                src_ref=source.at[edge, pl.ds(half * LANES, LANES)],
                dst_ref=image_ref.at[i, half, outer, :],
                send_sem=halo_sem.at[0, i, half],
                recv_sem=halo_sem.at[1, i, half],
                device_id={"rows": 1 - band},
                device_id_type=mesh_id,
            )
            halo.start()
            halos.append(halo)

    for load in loads[:3]:
        load.wait()
    index_vmem[...] = jnp.zeros(index_vmem.shape, jnp.int32)
    design_kernel(epochs_ref, slot_ref, coef_vmem, index_vmem, None, True)
    lane = lax.broadcasted_iota(jnp.int32, (1, LANES), 1)

    def place(k, held):
        cell = (offsets_ref[0, k] + SEARCH) * SIDE + offsets_ref[1, k] + SEARCH
        return jnp.where(lane == cell, k, held)

    index_vmem[1:2] = lax.fori_loop(0, count, place, jnp.full((1, LANES), count, jnp.int32), unroll=8)
    tables = [
        pltpu.make_async_copy(coef_vmem, coef_ref, table_sem.at[0]),
        pltpu.make_async_copy(index_vmem, index_ref, table_sem.at[1]),
    ]
    for move in tables:
        move.start()
    e_ref[count] = jnp.zeros(e_ref.shape[1:], jnp.float32)
    for load in loads[3:]:
        load.wait()
    prior_tables(
        lambda t: strided(prior_ref.at[0], t, steps),
        lambda t: strided(prior_ref.at[1], t, steps),
        a_ref,
        b_ref,
        pl.ds(0, columns),
    )
    for halo in halos:
        halo.wait()
    for move in tables:
        move.wait()
    prepare(image_ref, f_ref, s_ref, mean_ref, inv_ref, mean1_ref, inv1_ref)
    shift = lambda k: (offsets_ref[0, k] + SEARCH, offsets_ref[1, k] + SEARCH)
    correlate(shift, count, f_ref, s_ref, mean_ref, inv_ref, mean1_ref, inv1_ref, e_ref)

    def block(index):
        return pl.ds(pl.multiple_of(index * part, SUB), part)

    def push(phase, half, source, target):
        copies = []
        for i, peer in enumerate(peers):
            copy = pltpu.make_async_remote_copy(
                src_ref=source(peer),
                dst_ref=target(me),
                send_sem=send_sem.at[phase, half, i],
                recv_sem=recv_sem.at[phase, half, i],
                device_id={"pairs": peer},
                device_id_type=mesh_id,
            )
            copy.start()
            copies.append(copy)
        target(me)[...] = source(me)[...]
        return copies

    def finish(copies):
        for copy in copies:
            copy.wait()

    def match_half(phase, half):
        lanes = pl.ds(half * LANES, LANES)

        def store(t, row, col):
            field_ref[0, half, pl.ds(t, SUB, stride=steps), :] = row
            field_ref[1, half, pl.ds(t, SUB, stride=steps), :] = col

        cell = lambda i: index_ref[1, i]
        match_cells(cell, e_ref, a_ref, b_ref, lanes, 2 if steps % 2 == 0 else 1, store)
        return push(
            phase,
            half,
            lambda q: field_ref.at[:, half, block(q), :],
            lambda q: d_ref.at[phase // 2, half, q],
        )

    def invert_half(phase, half):
        sums = invert_segments(
            coef_ref,
            pairs,
            lambda p: d_ref[phase // 2, half, p],
            z_ref.at[half],
            g_ref.at[half],
            phase == 0,
        )
        if phase == 0:
            for p in range(pairs):
                gz_ref[half, p] = sums[p]
            return

        def expand(e, carry):
            plane = z_ref[half, index_ref[0, e]]
            for component in range(2):
                rows_of = pl.ds(half, part, stride=halves)
                velocity_ref[component, e, rows_of, :] = plane[component]
            return carry

        lax.fori_loop(0, EPOCHS, expand, 0, unroll=8)

    sent = [match_half(0, half) for half in range(halves)]
    returned = []
    for half in range(halves):
        finish(sent[half])
        invert_half(0, half)
        returned.append(
            push(
                1,
                half,
                lambda q: gz_ref.at[half, q],
                lambda q: back_ref.at[:, half, block(q), :],
            )
        )
    sent = []
    for half in range(halves):
        finish(returned[half])

        def prior(component):
            def at(t):
                place = pl.ds(t, SUB, stride=steps)
                given = prior_ref[component, half, place, :]
                return 0.5 * (given + back_ref[component, half, place, :])

            return at

        prior_tables(prior(0), prior(1), a_ref, b_ref, pl.ds(half * LANES, LANES))
        sent.append(match_half(2, half))
    for component in range(2):
        pieces = [field_ref[component, half] for half in range(halves)]
        motion_ref[component] = jnp.concatenate(pieces, axis=-1)
    for half in range(halves):
        finish(sent[half])
        invert_half(2, half)


def fused(first_image, second_image, prior, offsets, pair_epochs, pair_slot):
    rows, columns = first_image.shape
    steps, halves = rows // SUB, columns // LANES
    count, pairs = offsets.shape[0], pair_slot.shape[0]
    part = rows // pairs
    f32, i32 = jnp.float32, jnp.int32
    plane = (2, part, LANES)
    split = (2, halves, rows, LANES)
    dma = pltpu.SemaphoreType.DMA
    return pl.pallas_call(
        fused_kernel,
        out_shape=(
            jax.ShapeDtypeStruct((2, EPOCHS, part * halves, LANES), f32),
            jax.ShapeDtypeStruct((2, rows, columns), f32),
        ),
        in_specs=[pl.BlockSpec(memory_space=pltpu.HBM)] * 6,
        out_specs=(vmem_spec(), vmem_spec()),
        scratch_shapes=match_scratch(steps, columns)
        + weight_scratch(steps, columns)
        + [
            pltpu.VMEM((count + 1, steps, SUB, columns), f32),
            pltpu.VMEM(split, f32),
            pltpu.VMEM(split, f32),
            pltpu.VMEM((ROUNDS, halves, pairs) + plane, f32),
            pltpu.VMEM((halves, pairs) + plane, f32),
            pltpu.VMEM((halves, 2 * pairs + 1) + plane, f32),
            pltpu.VMEM((halves, pairs) + plane, f32),
            pltpu.VMEM((2 * pairs, LANES), f32),
            pltpu.VMEM((SUB, EPOCHS), i32),
            pltpu.SMEM((2 * pairs, LANES), f32),
            pltpu.SMEM((SUB, EPOCHS), i32),
            pltpu.SMEM((2, count), i32),
            pltpu.SMEM((2, pairs), i32),
            pltpu.SMEM((pairs,), i32),
            dma((3 + 4 * halves,)),
            dma((2,)),
            dma((2, 2, halves)),
            dma((3, halves, pairs)),
            dma((3, halves, pairs)),
        ],
        compiler_params=params(collective_id=0, has_side_effects=True),
        name="track",
    )(offsets.T, pair_epochs.T, pair_slot, first_image, second_image, prior)


def with_halo(cells, axis, dim, width):
    count = lax.axis_size(axis)
    head = lax.slice_in_dim(cells, 0, width, axis=dim)
    tail = lax.slice_in_dim(cells, cells.shape[dim] - width, cells.shape[dim], axis=dim)
    down = lax.ppermute(tail, axis, [(i, i + 1) for i in range(count - 1)])
    up = lax.ppermute(head, axis, [(i + 1, i) for i in range(count - 1)])
    return jnp.concatenate([down, cells, up], axis=dim)


def per_device(first_image, second_image, prior_motion, offsets, pair_epochs, pair_slot):
    rows, columns = first_image.shape[1:]
    steps = rows // SUB
    pairs = lax.axis_size("pairs")
    pixels = rows * columns // pairs
    fold = (pixels // LANES, LANES) if pixels % LANES == 0 else (1, pixels)
    f32 = functools.partial(jax.ShapeDtypeStruct, dtype=jnp.float32)
    prior = prior_motion[:, 0]
    whole_tiles = rows % (SUB * pairs) == 0 and columns % LANES == 0 and 2 * pairs <= LANES
    if whole_tiles and lax.axis_size("rows") == 2:
        velocity, motion = fused(
            first_image[0], second_image[0], prior, offsets, pair_epochs, pair_slot
        )
        return (velocity.reshape(2, EPOCHS, 1, pixels), motion[:, None])
    coef, seg, ends = design(pair_epochs, pair_slot)
    images = with_halo(jnp.concatenate((first_image, second_image), axis=0), "rows", 1, MARGIN)
    e, motion = pl.pallas_call(
        first_kernel,
        out_shape=(f32((offsets.shape[0], steps, SUB, columns)), f32((2, rows, columns))),
        in_specs=[smem_spec(), vmem_spec(), vmem_spec()],
        out_specs=(vmem_spec(), vmem_spec()),
        scratch_shapes=match_scratch(steps, columns) + weight_scratch(steps, columns),
        compiler_params=params(),
        name="correlate",
    )(offsets, images, prior)

    def spread(field):
        outgoing = field.reshape(2, 1, pairs, pixels)
        arrived = lax.all_to_all(outgoing, "pairs", split_axis=2, concat_axis=1, tiled=True)
        return arrived.reshape((2, pairs) + fold)

    def collect(field):
        outgoing = field.reshape(2, pairs, 1, pixels)
        arrived = lax.all_to_all(outgoing, "pairs", split_axis=1, concat_axis=2, tiled=True)
        return arrived.reshape(2, rows, columns)

    z_shape, g_shape = f32((2, EPOCHS) + fold), f32((2, pairs) + fold)
    tables = [
        pltpu.VMEM((2 * pairs + 1, 2) + fold, jnp.float32),
        pltpu.VMEM((EPOCHS + 1, 2) + fold, jnp.float32),
    ]
    small = [smem_spec()] * 3
    z, g, predicted = pl.pallas_call(
        invert_first_kernel,
        out_shape=(z_shape, g_shape, g_shape),
        in_specs=small + [vmem_spec()],
        out_specs=(vmem_spec(),) * 3,
        scratch_shapes=tables + [tables[1]],
        compiler_params=params(),
        name="invert_first",
    )(coef, seg, ends, spread(motion))
    motion = pl.pallas_call(
        again_kernel,
        out_shape=f32((2, rows, columns)),
        in_specs=[smem_spec()] + [vmem_spec()] * 3,
        out_specs=vmem_spec(),
        scratch_shapes=weight_scratch(steps, columns),
        compiler_params=params(),
        name="match_again",
    )(offsets, e, prior, collect(predicted))
    z, g = pl.pallas_call(
        invert_last_kernel,
        out_shape=(z_shape, g_shape),
        in_specs=small + [vmem_spec()] * 3,
        out_specs=(vmem_spec(),) * 2,
        scratch_shapes=tables,
        compiler_params=params(),
        name="invert_last",
    )(coef, seg, ends, spread(motion), z, g)
    return (z.reshape(2, EPOCHS, 1, pixels), motion[:, None])


def solution(mesh):
    placed = (
        P(("groups", "pairs"), "rows", None),
        P(("groups", "pairs"), "rows", None),
        P(None, ("groups", "pairs"), "rows", None),
        P(),
        P("groups", None),
        P("groups"),
    )
    return jax.shard_map(
        per_device,
        mesh=mesh,
        in_specs=placed,
        out_specs=(
            P(None, None, ("groups", "rows"), "pairs"),
            P(None, ("groups", "pairs"), "rows", None),
        ),
        check_vma=False,
    )
```

```python
import functools

import jax
import jax.numpy as jnp
from jax import lax
from jax.experimental import pallas as pl
from jax.experimental.pallas import tpu as pltpu
from jax.sharding import PartitionSpec as P

SEARCH = 4
RADIUS = 4
EPOCHS = 128
ITERS = 4
ROUNDS = 2

SOFTMIN_HEAT = 0.1
PRIOR_STRENGTH = 0.05
PENALTY = 4.0
SPARSITY = 0.4
VARIANCE_FLOOR = 0.05
HIGHEST = lax.Precision.HIGHEST

SIDE = 2 * SEARCH + 1
WINDOW = 2 * RADIUS + 1
MARGIN = SEARCH + RADIUS
SUB = 8
LANES = 128
AREA = 1.0 / float(WINDOW * WINDOW)
VMEM_BYTES = 64 * 1024 * 1024
BLOCK = 4
PIECES = 4


def vmem_spec():
    return pl.BlockSpec(memory_space=pltpu.VMEM)


def smem_spec():
    return pl.BlockSpec(memory_space=pltpu.SMEM)


def hbm_spec():
    return pl.BlockSpec(memory_space=pltpu.HBM)


def params(**more):
    return pltpu.CompilerParams(vmem_limit_bytes=VMEM_BYTES, **more)


def parts_of(values):
    high = values.astype(jnp.bfloat16)
    rest = values - high.astype(jnp.float32)
    middle = rest.astype(jnp.bfloat16)
    low = (rest - middle.astype(jnp.float32)).astype(jnp.bfloat16)
    return high, middle, low


def band_matrix(columns, shift):
    row = lax.broadcasted_iota(jnp.int32, (columns, columns), 0)
    col = lax.broadcasted_iota(jnp.int32, (columns, columns), 1)
    return (jnp.abs(row - col - shift) <= RADIUS).astype(jnp.float32).astype(jnp.bfloat16)


def column_box(values, band):
    parts = jnp.concatenate(parts_of(values), axis=1)
    bands = jnp.concatenate([band] * 3, axis=0)
    return jnp.dot(parts, bands, preferred_element_type=jnp.float32)


def row_box(planes, count):
    result = []
    for base in range(0, count, SUB):
        mid = base + WINDOW - 2
        suffix = {mid: planes[mid]}
        for i in range(mid - 1, base - 1, -1):
            suffix[i] = planes[i] + suffix[i + 1]
        prefix = {mid + 1: planes[mid + 1]}
        for i in range(mid + 2, base + SUB - 1 + WINDOW):
            prefix[i] = prefix[i - 1] + planes[i]
        for i in range(base, base + SUB):
            result.append(suffix[i] + prefix[i + WINDOW - 1])
    return result


def inverse_root(values):
    guess = lax.rsqrt(values)
    return guess * (1.5 - 0.5 * values * guess * guess)


def split_lanes(values):
    return jnp.stack([values[:, i : i + LANES] for i in range(0, values.shape[1], LANES)])


def strided(ref, start, stride):
    rows = pl.ds(start, SUB, stride=stride)
    return jnp.concatenate([ref[i, rows, :] for i in range(ref.shape[0])], axis=-1)


def store_strided(ref, start, stride, values):
    rows = pl.ds(start, SUB, stride=stride)
    for i in range(ref.shape[0]):
        ref[i, rows, :] = values[:, i * LANES : (i + 1) * LANES]


def prepare(image_ref, f_ref, s_ref, mean_ref, inv_ref, mean1_ref, inv1_ref):
    rows = image_ref.shape[2] - 2 * MARGIN
    columns = image_ref.shape[1] * LANES
    steps = rows // SUB
    band = band_matrix(columns, 0)

    raw = [strided(image_ref.at[0], SEARCH + t, steps) for t in range(steps + 2 * RADIUS)]
    scaled = [x * AREA for x in raw]
    for t, x in enumerate(scaled):
        f_ref[t] = x
    sums = row_box(scaled, steps) + row_box([a * b for a, b in zip(raw, scaled)], steps)
    boxed = column_box(jnp.concatenate(sums, axis=0), band)
    mean1 = boxed[:rows]
    var1 = boxed[rows:] - mean1 * mean1
    mean1_ref[...] = mean1.reshape(steps, SUB, columns)
    inv1 = inverse_root(jnp.maximum(var1, VARIANCE_FLOOR)) * (1.0 / SOFTMIN_HEAT)
    inv1_ref[...] = inv1.reshape(steps, SUB, columns)

    reach = steps + 2 * MARGIN
    second = [strided(image_ref.at[1], t, steps) for t in range(reach)]
    wide = steps + 2 * SEARCH
    sums = row_box(second, wide) + row_box([x * x for x in second], wide)
    sums = jnp.concatenate(parts_of(jnp.concatenate(sums, axis=0)), axis=1)
    stacked = jnp.concatenate(second, axis=0)
    lane = lax.broadcasted_iota(jnp.int32, stacked.shape, 1)
    half = wide * SUB
    for place in range(SIDE):
        shift = place - SEARCH
        moved = pltpu.roll(stacked, (-shift) % columns, 1) if shift else stacked
        inside = (lane + shift >= 0) & (lane + shift < columns)
        s_ref[place] = jnp.where(inside, moved, 0.0).reshape(reach, SUB, columns)
        shifted_band = band_matrix(columns, shift)
        bands = jnp.concatenate([shifted_band] * 3, axis=0)
        boxed = jnp.dot(sums, bands, preferred_element_type=jnp.float32) * AREA
        mean = boxed[:half]
        var = boxed[half:] - mean * mean
        mean_ref[place] = mean.reshape(wide, SUB, columns)
        inv = inverse_root(jnp.maximum(var, VARIANCE_FLOOR))
        inv_ref[place] = inv.reshape(wide, SUB, columns)


def correlate(shift, count, f_ref, s_ref, mean_ref, inv_ref, mean1_ref, inv1_ref, e_ref, side=None, held=None):
    steps, _, columns = mean1_ref.shape
    rows = steps * SUB
    band = band_matrix(columns, 0)
    block = BLOCK if count % BLOCK == 0 else 1

    def body(number, carry):
        sums = []
        for i in range(block):
            k = number * block + i
            oy, ox = shift(k)
            planes = [f_ref[t] * s_ref[ox, oy + t] for t in range(steps + 2 * RADIUS)]
            sums += row_box(planes, steps)
        boxed = column_box(jnp.concatenate(sums, axis=0), band)
        for i in range(block):
            k = number * block + i
            oy, ox = shift(k)
            for t in range(steps):
                at = i * rows + t * SUB
                cov = boxed[at : at + SUB] - mean1_ref[t] * mean_ref[ox, oy + t]
                e_ref[k, t] = jnp.exp(cov * (inv1_ref[t] * inv_ref[ox, oy + t]))
        return carry if side is None else side(number, carry)

    return count // block, lax.fori_loop(0, count // block, body, 0 if side is None else held)


def prior_tables(prior_row, prior_col, a_ref, b_ref, lanes):
    steps = a_ref.shape[1]
    curve = 0.5 * (2.0 * PRIOR_STRENGTH / SOFTMIN_HEAT)
    for t in range(steps):
        for ref, prior in ((a_ref, prior_row(t)), (b_ref, prior_col(t))):
            near = jnp.clip(jnp.floor(prior + 0.5), -float(SEARCH), float(SEARCH))
            twice = near - 2.0 * prior
            for place in range(SIDE):
                i = float(place - SEARCH)
                ref[place, t, :, lanes] = jnp.exp(curve * ((near - i) * (twice + i)))


def match(offsets_ref, e_ref, a_ref, b_ref, lanes, together, store):
    count, steps = e_ref.shape[:2]
    for base in range(0, steps, together):
        here = pl.ds(base, together)
        zero = jnp.zeros((together, SUB, lanes.size), jnp.float32)

        def body(k, carry):
            total, rows, cols = carry
            oy = offsets_ref[k, 0]
            ox = offsets_ref[k, 1]
            table = a_ref[oy + SEARCH, here, :, lanes] * b_ref[ox + SEARCH, here, :, lanes]
            weight = e_ref[k, here, :, lanes] * table
            return (
                total + weight,
                rows + weight * oy.astype(jnp.float32),
                cols + weight * ox.astype(jnp.float32),
            )

        total, rows, cols = lax.fori_loop(0, count, body, (zero, zero, zero), unroll=8)
        for i in range(together):
            store(base + i, rows[i] / total[i], cols[i] / total[i])


def match_cells(cell, e_ref, a_ref, b_ref, lanes, together, store):
    steps = e_ref.shape[1]
    for base in range(0, steps, together):
        here = pl.ds(base, together)
        zero = jnp.zeros((together, SUB, lanes.size), jnp.float32)
        table = [b_ref[j, here, :, lanes] for j in range(SIDE)]
        moment = [x * float(j - SEARCH) for j, x in enumerate(table)]

        def body(i, carry):
            total, rows, cols = carry
            first, second = zero, zero
            for j in range(SIDE):
                e = e_ref[cell(i * SIDE + j), here, :, lanes]
                first = first + e * table[j]
                if j != SEARCH:
                    second = second + e * moment[j]
            a = a_ref[i, here, :, lanes]
            weight = a * first
            shift = lax.convert_element_type(i - SEARCH, jnp.float32)
            return total + weight, rows + weight * shift, cols + a * second

        total, rows, cols = lax.fori_loop(0, SIDE, body, (zero, zero, zero), unroll=True)
        for i in range(together):
            store(base + i, rows[i] / total[i], cols[i] / total[i])


def eliminate(j, a):
    row_id = lax.broadcasted_iota(jnp.int32, a.shape, 0)
    col_id = lax.broadcasted_iota(jnp.int32, a.shape, 1)
    on_row = row_id == j
    on_col = col_id == j
    row = jnp.sum(jnp.where(on_row, a, 0.0), axis=0, keepdims=True)
    col = jnp.sum(jnp.where(on_col, a, 0.0), axis=1, keepdims=True)
    pivot = jnp.sum(jnp.where(col_id[:1] == j, row, 0.0), axis=1, keepdims=True)
    scale = jnp.where(j < a.shape[0], 1.0 / pivot, 0.0)
    inner = a - col * (row * scale)
    return jnp.where(
        on_row,
        jnp.where(on_col, scale, row * scale),
        jnp.where(on_col, -col * scale, inner),
    )


def design_begin(epochs_ref, slot_ref, ends_ref):
    pairs = slot_ref.shape[0]
    ends = 2 * pairs
    row_id = lax.broadcasted_iota(jnp.int32, (pairs, pairs), 0)
    col_id = lax.broadcasted_iota(jnp.int32, (pairs, pairs), 1)
    end_id = lax.broadcasted_iota(jnp.int32, (ends, pairs), 0)
    end_col = lax.broadcasted_iota(jnp.int32, (ends, pairs), 1)
    seg_id = lax.broadcasted_iota(jnp.int32, (ends, EPOCHS), 0)

    def gather(j, state):
        first_r, after_r, first_c, after_c, mark, mark_e, first_e, after_e = state
        first = epochs_ref[0, slot_ref[j]]
        after = epochs_ref[1, slot_ref[j]]
        if ends_ref is not None:
            ends_ref[0, j] = first
            ends_ref[1, j] = after
        return (
            jnp.where(row_id == j, first, first_r),
            jnp.where(row_id == j, after, after_r),
            jnp.where(col_id == j, first, first_c),
            jnp.where(col_id == j, after, after_c),
            jnp.where(end_id == j, first, jnp.where(end_id == j + pairs, after, mark)),
            jnp.where(seg_id == j, first, jnp.where(seg_id == j + pairs, after, mark_e)),
            jnp.where(end_col == j, first, first_e),
            jnp.where(end_col == j, after, after_e),
        )

    square = jnp.zeros((pairs, pairs), jnp.int32)
    tall = jnp.zeros((ends, pairs), jnp.int32)
    state = (square, square, square, square, tall, jnp.zeros((ends, EPOCHS), jnp.int32), tall, tall)
    first_r, after_r, first_c, after_c, mark, mark_e, first_e, after_e = lax.fori_loop(
        0, pairs, gather, state
    )
    overlap = jnp.maximum(jnp.minimum(after_r, after_c) - jnp.maximum(first_r, first_c), 0)
    matrix = overlap.astype(jnp.float32) + jnp.where(row_id == col_id, PENALTY, 0.0)

    inside = ((mark >= first_e) & (mark < after_e)).astype(jnp.float32)
    return matrix, (inside, mark_e)


def design_end(inverse, intervals, coef_ref, seg_ref, weigh=False):
    inside, mark_e = intervals
    ends = inside.shape[0]
    seg_id = lax.broadcasted_iota(jnp.int32, (ends, EPOCHS), 0)
    epoch = lax.broadcasted_iota(jnp.int32, (ends, EPOCHS), 1)
    latest = jnp.max(jnp.where(mark_e <= epoch, mark_e, -1), axis=0, keepdims=True)
    which = jnp.max(jnp.where(mark_e == latest, seg_id, -1), axis=0, keepdims=True)
    which = jnp.where(latest < 0, ends, which)
    seg_ref[0:1] = which
    coef = jnp.dot(inside, inverse, precision=HIGHEST, preferred_element_type=jnp.float32)
    if weigh:
        long = jnp.sum((which == seg_id).astype(jnp.float32), axis=1, keepdims=True)
        blank = jnp.zeros((ends, coef_ref.shape[1] - ends), jnp.float32)
        coef = jnp.concatenate([coef, inside * long, blank], axis=1)
    coef_ref[...] = coef


def design_kernel(epochs_ref, slot_ref, coef_ref, seg_ref, ends_ref):
    matrix, intervals = design_begin(epochs_ref, slot_ref, ends_ref)
    inverse = lax.fori_loop(0, slot_ref.shape[0], eliminate, matrix)
    design_end(inverse, intervals, coef_ref, seg_ref)


def design(pair_epochs, pair_slot):
    pairs = pair_slot.shape[0]
    return pl.pallas_call(
        design_kernel,
        out_shape=(
            jax.ShapeDtypeStruct((2 * pairs, pairs), jnp.float32),
            jax.ShapeDtypeStruct((1, EPOCHS), jnp.int32),
            jax.ShapeDtypeStruct((2, pairs), jnp.int32),
        ),
        in_specs=[smem_spec(), smem_spec()],
        out_specs=(vmem_spec(), vmem_spec(), smem_spec()),
        compiler_params=params(),
        name="design",
    )(pair_epochs.T, pair_slot)


def invert(coef_ref, seg_ref, ends_ref, pairs, d, begin, z, g, t_ref, cum_ref, predict):
    ends = 2 * pairs
    threshold = SPARSITY / PENALTY
    zero = jnp.zeros(t_ref.shape[1:], jnp.float32)
    t_ref[ends] = zero
    cum_ref[0] = zero
    if predict is not None:
        predict[1][0] = zero
    short = pairs <= 16

    for iteration in range(ITERS):
        start = begin is None and iteration == 0
        z_from, g_from = begin if begin and iteration == 0 else (z[0], g[0])
        last = iteration + 1 == ITERS
        summing = last and predict is not None

        def residual(p):
            return d(p) if start else d(p) - g_from(p)

        if short:
            gaps = [residual(p) for p in range(pairs)]
            for j in range(ends):
                value = coef_ref[j, 0] * gaps[0]
                for p in range(1, pairs):
                    value = value + coef_ref[j, p] * gaps[p]
                t_ref[j] = value
        else:

            def fill(j):
                t_ref[j] = lax.fori_loop(
                    0, pairs, lambda p, v: v + coef_ref[j, p] * residual(p), zero
                )

            pl.loop(0, ends)(fill)

        def epoch_step(e, carry):
            s = t_ref[seg_ref[0, e]]
            if not start:
                s = s + z_from(e)
            u = jnp.clip(s, -threshold, threshold)
            new = s - u
            z[1](e, new, last)
            if last and not summing:
                return carry
            run = carry[0] + (new - u)
            cum_ref[e + 1] = run
            if not summing:
                return (run,)
            run_z = carry[1] + new
            predict[1][e + 1] = run_z
            return (run, run_z)

        lax.fori_loop(0, EPOCHS, epoch_step, (zero, zero) if summing else (zero,), unroll=8)
        if last and not summing:
            return

        def collect(p):
            first, after = ends_ref[0, p], ends_ref[1, p]
            g[1](p, cum_ref[after] - cum_ref[first])
            if summing:
                predict[0](p, predict[1][after] - predict[1][first])

        if short:
            for p in range(pairs):
                collect(p)
        else:
            pl.loop(0, pairs)(collect)


def invert_segments(coef_ref, pairs, d, z_ref, g_ref, fresh):
    ends = 2 * pairs
    threshold = SPARSITY / PENALTY
    zero = jnp.zeros(z_ref.shape[1:], jnp.float32)
    if fresh:
        for j in range(ends + 1):
            z_ref[j] = zero
    seen = [d(p) for p in range(pairs)]

    def weigh(j, value, sums):
        return tuple(g + coef_ref[j, pairs + p] * value for p, g in enumerate(sums))

    def step(iteration, held):
        gaps = [a - b for a, b in zip(seen, held)]
        sums = (zero,) * pairs
        for j in range(ends):
            terms = [coef_ref[j, p] * gap for p, gap in enumerate(gaps)]
            while len(terms) > 1:
                terms = [sum(terms[i : i + 2][1:], terms[i]) for i in range(0, len(terms), 2)]
            s = z_ref[j] + terms[0]
            u = jnp.clip(s, -threshold, threshold)
            z = s - u
            z_ref[j] = z
            sums = weigh(j, z - u, sums)
        return sums

    held = (zero,) * pairs if fresh else tuple(g_ref[p] for p in range(pairs))
    held = lax.fori_loop(0, ITERS, step, held)
    if not fresh:
        return None
    for p in range(pairs):
        g_ref[p] = held[p]
    sums = (zero,) * pairs
    for j in range(ends):
        sums = weigh(j, z_ref[j], sums)
    return sums


def second_axis(ref):
    def store(i, value, last=False):
        ref[:, i] = value

    return (lambda i: ref[:, i]), store


def match_scratch(steps, columns):
    plane = (SUB, columns)
    extended = (2, columns // LANES, steps * SUB + 2 * MARGIN, LANES)
    return [
        pltpu.VMEM(extended, jnp.float32),
        pltpu.VMEM((steps + 2 * RADIUS,) + plane, jnp.float32),
        pltpu.VMEM((SIDE, steps + 2 * MARGIN) + plane, jnp.float32),
        pltpu.VMEM((SIDE, steps + 2 * SEARCH) + plane, jnp.float32),
        pltpu.VMEM((SIDE, steps + 2 * SEARCH) + plane, jnp.float32),
        pltpu.VMEM((steps,) + plane, jnp.float32),
        pltpu.VMEM((steps,) + plane, jnp.float32),
    ]


def weight_scratch(steps, columns):
    tables = [pltpu.VMEM((SIDE, steps, SUB, columns), jnp.float32)] * 2
    return tables + [pltpu.VMEM((2, columns // LANES, steps * SUB, LANES), jnp.float32)]


def match_on(offsets_ref, e_ref, prior_ref, back_ref, a_ref, b_ref, field_ref, motion_ref):
    steps = e_ref.shape[1]
    for component in range(2):
        values = prior_ref[component]
        if back_ref is not None:
            values = 0.5 * (values + back_ref[component])
        field_ref[component] = split_lanes(values)

    def prior(component):
        return lambda t: strided(field_ref.at[component], t, steps)

    def store(t, row, col):
        store_strided(field_ref.at[0], t, steps, row)
        store_strided(field_ref.at[1], t, steps, col)

    lanes = pl.ds(0, e_ref.shape[3])
    prior_tables(prior(0), prior(1), a_ref, b_ref, lanes)
    match(offsets_ref, e_ref, a_ref, b_ref, lanes, 2, store)
    for component in range(2):
        halves = [field_ref[component, i] for i in range(field_ref.shape[1])]
        motion_ref[component] = jnp.concatenate(halves, axis=-1)


def first_kernel(offsets_ref, images_ref, prior_ref, e_ref, motion_ref, *scratch):
    image_ref, *tables = scratch[:7]
    for i in range(2):
        image_ref[i] = split_lanes(images_ref[i])
    prepare(image_ref, *tables)
    shift = lambda k: (offsets_ref[k, 0] + SEARCH, offsets_ref[k, 1] + SEARCH)
    correlate(shift, offsets_ref.shape[0], *tables, e_ref)
    match_on(offsets_ref, e_ref, prior_ref, None, *scratch[7:], motion_ref)


def again_kernel(offsets_ref, e_ref, prior_ref, back_ref, motion_ref, *scratch):
    match_on(offsets_ref, e_ref, prior_ref, back_ref, *scratch, motion_ref)


def invert_first_kernel(coef_ref, seg_ref, ends_ref, d_ref, z_ref, g_ref, gz_ref, t_ref, cum_ref, cumz_ref):
    z, g, d, gz = (second_axis(ref) for ref in (z_ref, g_ref, d_ref, gz_ref))
    tables = (coef_ref, seg_ref, ends_ref, d_ref.shape[1])
    invert(*tables, d[0], None, z, g, t_ref, cum_ref, (gz[1], cumz_ref))


def invert_last_kernel(coef_ref, seg_ref, ends_ref, d_ref, zin_ref, gin_ref, z_ref, g_ref, t_ref, cum_ref):
    z, g, d = (second_axis(ref) for ref in (z_ref, g_ref, d_ref))
    begin = (second_axis(zin_ref)[0], second_axis(gin_ref)[0])
    tables = (coef_ref, seg_ref, ends_ref, d_ref.shape[1])
    invert(*tables, d[0], begin, z, g, t_ref, cum_ref, None)


def fused_kernel(
    offsets_hbm,
    epochs_hbm,
    slot_hbm,
    first_hbm,
    second_hbm,
    prior_hbm,
    z_ref,
    index_vmem,
    motion_ref,
    image_ref,
    f_ref,
    s_ref,
    mean_ref,
    inv_ref,
    mean1_ref,
    inv1_ref,
    a_ref,
    b_ref,
    field_ref,
    e_ref,
    prior_ref,
    back_ref,
    d_ref,
    gz_ref,
    g_ref,
    coef_vmem,
    coef_ref,
    index_ref,
    offsets_ref,
    epochs_ref,
    slot_ref,
    load_sem,
    table_sem,
    halo_sem,
    send_sem,
    recv_sem,
):
    rows, columns = first_hbm.shape
    steps = rows // SUB
    halves = columns // LANES
    pairs = slot_ref.shape[0]
    part = rows // pairs
    count = offsets_ref.shape[1]
    me = lax.axis_index("pairs")
    band = lax.axis_index("rows")
    mesh_id = pl.DeviceIdType.MESH

    barrier = pltpu.get_barrier_semaphore()
    peers = [lax.rem(me + i, pairs) for i in range(1, pairs)]
    pl.semaphore_signal(barrier, inc=1, device_id={"rows": 1 - band}, device_id_type=mesh_id)
    for peer in peers:
        pl.semaphore_signal(barrier, inc=1, device_id={"pairs": peer}, device_id_type=mesh_id)

    moves = [(epochs_hbm, epochs_ref), (slot_hbm, slot_ref), (offsets_hbm, offsets_ref)]
    for half in range(halves):
        lanes = pl.ds(half * LANES, LANES)
        inner = pl.ds(MARGIN, rows)
        moves += [
            (prior_hbm.at[0, :, lanes], prior_ref.at[0, half]),
            (prior_hbm.at[1, :, lanes], prior_ref.at[1, half]),
            (first_hbm.at[:, lanes], image_ref.at[0, half, inner]),
            (second_hbm.at[:, lanes], image_ref.at[1, half, inner]),
        ]
    loads = [
        pltpu.make_async_copy(source, target, load_sem.at[i])
        for i, (source, target) in enumerate(moves)
    ]
    for load in loads:
        load.start()
    outer = pl.ds(pl.multiple_of(band * (rows + MARGIN), SUB), MARGIN)
    edge = pl.ds(pl.multiple_of((1 - band) * (rows - MARGIN), SUB), MARGIN)
    image_ref[:, :, outer, :] = jnp.zeros((2, halves, MARGIN, LANES), jnp.float32)
    pl.semaphore_wait(barrier, pairs)
    halos = []
    for i, source in enumerate((first_hbm, second_hbm)):
        for half in range(halves):
            halo = pltpu.make_async_remote_copy(
                src_ref=source.at[edge, pl.ds(half * LANES, LANES)],
                dst_ref=image_ref.at[i, half, outer, :],
                send_sem=halo_sem.at[0, i, half],
                recv_sem=halo_sem.at[1, i, half],
                device_id={"rows": 1 - band},
                device_id_type=mesh_id,
            )
            halo.start()
            halos.append(halo)

    for load in loads[:3]:
        load.wait()
    index_vmem[...] = jnp.zeros(index_vmem.shape, jnp.int32)
    matrix, intervals = design_begin(epochs_ref, slot_ref, None)
    lane = lax.broadcasted_iota(jnp.int32, (1, LANES), 1)

    def place(k, held):
        cell = (offsets_ref[0, k] + SEARCH) * SIDE + offsets_ref[1, k] + SEARCH
        return jnp.where(lane == cell, k, held)

    index_vmem[1:2] = lax.fori_loop(0, count, place, jnp.full((1, LANES), count, jnp.int32), unroll=8)
    e_ref[count] = jnp.zeros(e_ref.shape[1:], jnp.float32)
    for load in loads[3:]:
        load.wait()
    prior_tables(
        lambda t: strided(prior_ref.at[0], t, steps),
        lambda t: strided(prior_ref.at[1], t, steps),
        a_ref,
        b_ref,
        pl.ds(0, columns),
    )
    for halo in halos:
        halo.wait()
    prepare(image_ref, f_ref, s_ref, mean_ref, inv_ref, mean1_ref, inv1_ref)
    shift = lambda k: (offsets_ref[0, k] + SEARCH, offsets_ref[1, k] + SEARCH)
    images = (f_ref, s_ref, mean_ref, inv_ref, mean1_ref, inv1_ref)
    done, matrix = correlate(shift, count, *images, e_ref, eliminate, matrix)
    inverse = lax.fori_loop(done, max(done, pairs), eliminate, matrix) if done < pairs else matrix
    design_end(inverse, intervals, coef_vmem, index_vmem, True)
    tables = [
        pltpu.make_async_copy(coef_vmem, coef_ref, table_sem.at[0]),
        pltpu.make_async_copy(index_vmem, index_ref, table_sem.at[1]),
    ]
    for move in tables:
        move.start()
    for move in tables:
        move.wait()

    def block(index):
        return pl.ds(pl.multiple_of(index * part, SUB), part)

    def push(phase, half, source, target):
        copies = []
        for i, peer in enumerate(peers):
            copy = pltpu.make_async_remote_copy(
                src_ref=source(peer),
                dst_ref=target(me),
                send_sem=send_sem.at[phase, half, i],
                recv_sem=recv_sem.at[phase, half, i],
                device_id={"pairs": peer},
                device_id_type=mesh_id,
            )
            copy.start()
            copies.append(copy)
        target(me)[...] = source(me)[...]
        return copies

    def finish(copies):
        for copy in copies:
            copy.wait()

    def match_half(phase, half):
        lanes = pl.ds(half * LANES, LANES)

        def store(t, row, col):
            field_ref[0, half, pl.ds(t, SUB, stride=steps), :] = row
            field_ref[1, half, pl.ds(t, SUB, stride=steps), :] = col

        cell = lambda i: index_ref[1, i]
        match_cells(cell, e_ref, a_ref, b_ref, lanes, 2 if steps % 2 == 0 else 1, store)
        return push(
            phase,
            half,
            lambda q: field_ref.at[:, half, block(q), :],
            lambda q: d_ref.at[phase // 2, half, q],
        )

    def invert_half(phase, half):
        sums = invert_segments(
            coef_ref,
            pairs,
            lambda p: d_ref[phase // 2, half, p],
            z_ref.at[half],
            g_ref.at[half],
            phase == 0,
        )
        if phase == 0:
            for p in range(pairs):
                gz_ref[half, p] = sums[p]
            return

    sent = [match_half(0, half) for half in range(halves)]
    returned = []
    for half in range(halves):
        finish(sent[half])
        invert_half(0, half)
        returned.append(
            push(
                1,
                half,
                lambda q: gz_ref.at[half, q],
                lambda q: back_ref.at[:, half, block(q), :],
            )
        )
    sent = []
    for half in range(halves):
        finish(returned[half])

        def prior(component):
            def at(t):
                place = pl.ds(t, SUB, stride=steps)
                given = prior_ref[component, half, place, :]
                return 0.5 * (given + back_ref[component, half, place, :])

            return at

        prior_tables(prior(0), prior(1), a_ref, b_ref, pl.ds(half * LANES, LANES))
        sent.append(match_half(2, half))
    for component in range(2):
        pieces = [field_ref[component, half] for half in range(halves)]
        motion_ref[component] = jnp.concatenate(pieces, axis=-1)
    for half in range(halves):
        finish(sent[half])
        invert_half(2, half)


def expand_kernel(z_hbm, index_hbm, motion_hbm, velocity_hbm, out_hbm, z_ref, index_ref, velocity_ref, sem, out_sem):
    halves, part = z_ref.shape[0], z_ref.shape[3]
    moves = [
        pltpu.make_async_copy(z_hbm, z_ref, sem.at[0]),
        pltpu.make_async_copy(index_hbm, index_ref, sem.at[1]),
        pltpu.make_async_copy(motion_hbm, out_hbm, sem.at[2]),
    ]
    for move in moves:
        move.start()
    moves[0].wait()
    moves[1].wait()
    length = EPOCHS // PIECES
    outs = []
    for piece in range(PIECES):

        def expand(i, carry):
            e = piece * length + i
            segment = index_ref[0, e]
            for half in range(halves):
                plane = z_ref[half, segment]
                for component in range(2):
                    velocity_ref[component, e, pl.ds(half, part, stride=halves), :] = plane[component]
            return carry

        lax.fori_loop(0, length, expand, 0, unroll=8)
        for component in range(2):
            here = (component, pl.ds(piece * length, length))
            out = pltpu.make_async_copy(
                velocity_ref.at[here], velocity_hbm.at[here], out_sem.at[component, piece]
            )
            out.start()
            outs.append(out)
    for out in outs:
        out.wait()
    moves[2].wait()


def fused(first_image, second_image, prior, offsets, pair_epochs, pair_slot):
    rows, columns = first_image.shape
    steps, halves = rows // SUB, columns // LANES
    count, pairs = offsets.shape[0], pair_slot.shape[0]
    part = rows // pairs
    f32, i32 = jnp.float32, jnp.int32
    plane = (2, part, LANES)
    split = (2, halves, rows, LANES)
    dma = pltpu.SemaphoreType.DMA
    z, index, motion = pl.pallas_call(
        fused_kernel,
        out_shape=(
            jax.ShapeDtypeStruct((halves, 2 * pairs + 1) + plane, f32),
            jax.ShapeDtypeStruct((SUB, EPOCHS), i32),
            jax.ShapeDtypeStruct((2, rows, columns), f32),
        ),
        in_specs=[hbm_spec()] * 6,
        out_specs=(vmem_spec(),) * 3,
        scratch_shapes=match_scratch(steps, columns)
        + weight_scratch(steps, columns)
        + [
            pltpu.VMEM((count + 1, steps, SUB, columns), f32),
            pltpu.VMEM(split, f32),
            pltpu.VMEM(split, f32),
            pltpu.VMEM((ROUNDS, halves, pairs) + plane, f32),
            pltpu.VMEM((halves, pairs) + plane, f32),
            pltpu.VMEM((halves, pairs) + plane, f32),
            pltpu.VMEM((2 * pairs, LANES), f32),
            pltpu.SMEM((2 * pairs, LANES), f32),
            pltpu.SMEM((SUB, EPOCHS), i32),
            pltpu.SMEM((2, count), i32),
            pltpu.SMEM((2, pairs), i32),
            pltpu.SMEM((pairs,), i32),
            dma((3 + 4 * halves,)),
            dma((2,)),
            dma((2, 2, halves)),
            dma((3, halves, pairs)),
            dma((3, halves, pairs)),
        ],
        compiler_params=params(collective_id=0, has_side_effects=True),
        name="track",
    )(offsets.T, pair_epochs.T, pair_slot, first_image, second_image, prior)
    whole = (2, EPOCHS, part * halves, LANES)
    return pl.pallas_call(
        expand_kernel,
        out_shape=(
            jax.ShapeDtypeStruct(whole, f32),
            jax.ShapeDtypeStruct((2, rows, columns), f32),
        ),
        in_specs=[hbm_spec()] * 3,
        out_specs=(hbm_spec(),) * 2,
        scratch_shapes=[
            pltpu.VMEM(z.shape, f32),
            pltpu.SMEM(index.shape, i32),
            pltpu.VMEM(whole, f32),
            dma((3,)),
            dma((2, PIECES)),
        ],
        compiler_params=params(),
        name="expand",
    )(z, index, motion)


def with_halo(cells, axis, dim, width):
    count = lax.axis_size(axis)
    head = lax.slice_in_dim(cells, 0, width, axis=dim)
    tail = lax.slice_in_dim(cells, cells.shape[dim] - width, cells.shape[dim], axis=dim)
    down = lax.ppermute(tail, axis, [(i, i + 1) for i in range(count - 1)])
    up = lax.ppermute(head, axis, [(i + 1, i) for i in range(count - 1)])
    return jnp.concatenate([down, cells, up], axis=dim)


def per_device(first_image, second_image, prior_motion, offsets, pair_epochs, pair_slot):
    rows, columns = first_image.shape[1:]
    steps = rows // SUB
    pairs = lax.axis_size("pairs")
    pixels = rows * columns // pairs
    fold = (pixels // LANES, LANES) if pixels % LANES == 0 else (1, pixels)
    f32 = functools.partial(jax.ShapeDtypeStruct, dtype=jnp.float32)
    prior = prior_motion[:, 0]
    whole_tiles = rows % (SUB * pairs) == 0 and columns % LANES == 0 and 2 * pairs <= LANES
    if whole_tiles and lax.axis_size("rows") == 2:
        velocity, motion = fused(
            first_image[0], second_image[0], prior, offsets, pair_epochs, pair_slot
        )
        return (velocity.reshape(2, EPOCHS, 1, pixels), motion[:, None])
    coef, seg, ends = design(pair_epochs, pair_slot)
    images = with_halo(jnp.concatenate((first_image, second_image), axis=0), "rows", 1, MARGIN)
    e, motion = pl.pallas_call(
        first_kernel,
        out_shape=(f32((offsets.shape[0], steps, SUB, columns)), f32((2, rows, columns))),
        in_specs=[smem_spec(), vmem_spec(), vmem_spec()],
        out_specs=(vmem_spec(), vmem_spec()),
        scratch_shapes=match_scratch(steps, columns) + weight_scratch(steps, columns),
        compiler_params=params(),
        name="correlate",
    )(offsets, images, prior)

    def spread(field):
        outgoing = field.reshape(2, 1, pairs, pixels)
        arrived = lax.all_to_all(outgoing, "pairs", split_axis=2, concat_axis=1, tiled=True)
        return arrived.reshape((2, pairs) + fold)

    def collect(field):
        outgoing = field.reshape(2, pairs, 1, pixels)
        arrived = lax.all_to_all(outgoing, "pairs", split_axis=1, concat_axis=2, tiled=True)
        return arrived.reshape(2, rows, columns)

    z_shape, g_shape = f32((2, EPOCHS) + fold), f32((2, pairs) + fold)
    tables = [
        pltpu.VMEM((2 * pairs + 1, 2) + fold, jnp.float32),
        pltpu.VMEM((EPOCHS + 1, 2) + fold, jnp.float32),
    ]
    small = [smem_spec()] * 3
    z, g, predicted = pl.pallas_call(
        invert_first_kernel,
        out_shape=(z_shape, g_shape, g_shape),
        in_specs=small + [vmem_spec()],
        out_specs=(vmem_spec(),) * 3,
        scratch_shapes=tables + [tables[1]],
        compiler_params=params(),
        name="invert_first",
    )(coef, seg, ends, spread(motion))
    motion = pl.pallas_call(
        again_kernel,
        out_shape=f32((2, rows, columns)),
        in_specs=[smem_spec()] + [vmem_spec()] * 3,
        out_specs=vmem_spec(),
        scratch_shapes=weight_scratch(steps, columns),
        compiler_params=params(),
        name="match_again",
    )(offsets, e, prior, collect(predicted))
    z, g = pl.pallas_call(
        invert_last_kernel,
        out_shape=(z_shape, g_shape),
        in_specs=small + [vmem_spec()] * 3,
        out_specs=(vmem_spec(),) * 2,
        scratch_shapes=tables,
        compiler_params=params(),
        name="invert_last",
    )(coef, seg, ends, spread(motion), z, g)
    return (z.reshape(2, EPOCHS, 1, pixels), motion[:, None])


def solution(mesh):
    placed = (
        P(("groups", "pairs"), "rows", None),
        P(("groups", "pairs"), "rows", None),
        P(None, ("groups", "pairs"), "rows", None),
        P(),
        P("groups", None),
        P("groups"),
    )
    return jax.shard_map(
        per_device,
        mesh=mesh,
        in_specs=placed,
        out_specs=(
            P(None, None, ("groups", "rows"), "pairs"),
            P(None, ("groups", "pairs"), "rows", None),
        ),
        check_vma=False,
    )
```

```python
import functools

import jax
import jax.numpy as jnp
from jax import lax
from jax.experimental import pallas as pl
from jax.experimental.pallas import tpu as pltpu
from jax.sharding import PartitionSpec as P

SEARCH = 4
RADIUS = 4
EPOCHS = 128
ITERS = 4
ROUNDS = 2

SOFTMIN_HEAT = 0.1
PRIOR_STRENGTH = 0.05
PENALTY = 4.0
SPARSITY = 0.4
VARIANCE_FLOOR = 0.05
HIGHEST = lax.Precision.HIGHEST

SIDE = 2 * SEARCH + 1
WINDOW = 2 * RADIUS + 1
MARGIN = SEARCH + RADIUS
SUB = 8
LANES = 128
AREA = 1.0 / float(WINDOW * WINDOW)
VMEM_BYTES = 64 * 1024 * 1024
BLOCK = 8
PIECES = 4


def vmem_spec():
    return pl.BlockSpec(memory_space=pltpu.VMEM)


def smem_spec():
    return pl.BlockSpec(memory_space=pltpu.SMEM)


def hbm_spec():
    return pl.BlockSpec(memory_space=pltpu.HBM)


def params(**more):
    return pltpu.CompilerParams(vmem_limit_bytes=VMEM_BYTES, **more)


def parts_of(values):
    high = values.astype(jnp.bfloat16)
    rest = values - high.astype(jnp.float32)
    middle = rest.astype(jnp.bfloat16)
    low = (rest - middle.astype(jnp.float32)).astype(jnp.bfloat16)
    return high, middle, low


def band_matrix(columns, shift):
    row = lax.broadcasted_iota(jnp.int32, (columns, columns), 0)
    col = lax.broadcasted_iota(jnp.int32, (columns, columns), 1)
    return (jnp.abs(row - col - shift) <= RADIUS).astype(jnp.float32).astype(jnp.bfloat16)


def column_box(values, band):
    parts = jnp.concatenate(parts_of(values), axis=1)
    bands = jnp.concatenate([band] * 3, axis=0)
    return jnp.dot(parts, bands, preferred_element_type=jnp.float32)


def row_box(planes, count):
    result = []
    for base in range(0, count, SUB):
        mid = base + WINDOW - 2
        suffix = {mid: planes[mid]}
        for i in range(mid - 1, base - 1, -1):
            suffix[i] = planes[i] + suffix[i + 1]
        prefix = {mid + 1: planes[mid + 1]}
        for i in range(mid + 2, base + SUB - 1 + WINDOW):
            prefix[i] = prefix[i - 1] + planes[i]
        for i in range(base, base + SUB):
            result.append(suffix[i] + prefix[i + WINDOW - 1])
    return result


def inverse_root(values):
    guess = lax.rsqrt(values)
    return guess * (1.5 - 0.5 * values * guess * guess)


def split_lanes(values):
    return jnp.stack([values[:, i : i + LANES] for i in range(0, values.shape[1], LANES)])


def strided(ref, start, stride):
    rows = pl.ds(start, SUB, stride=stride)
    return jnp.concatenate([ref[i, rows, :] for i in range(ref.shape[0])], axis=-1)


def store_strided(ref, start, stride, values):
    rows = pl.ds(start, SUB, stride=stride)
    for i in range(ref.shape[0]):
        ref[i, rows, :] = values[:, i * LANES : (i + 1) * LANES]


def prepare(image_ref, f_ref, s_ref, mean_ref, inv_ref, mean1_ref, inv1_ref):
    rows = image_ref.shape[2] - 2 * MARGIN
    columns = image_ref.shape[1] * LANES
    steps = rows // SUB
    band = band_matrix(columns, 0)

    raw = [strided(image_ref.at[0], SEARCH + t, steps) for t in range(steps + 2 * RADIUS)]
    scaled = [x * AREA for x in raw]
    for t, x in enumerate(scaled):
        f_ref[t] = x
    sums = row_box(scaled, steps) + row_box([a * b for a, b in zip(raw, scaled)], steps)
    boxed = column_box(jnp.concatenate(sums, axis=0), band)
    mean1 = boxed[:rows]
    var1 = boxed[rows:] - mean1 * mean1
    mean1_ref[...] = mean1.reshape(steps, SUB, columns)
    inv1 = inverse_root(jnp.maximum(var1, VARIANCE_FLOOR)) * (1.0 / SOFTMIN_HEAT)
    inv1_ref[...] = inv1.reshape(steps, SUB, columns)

    reach = steps + 2 * MARGIN
    second = [strided(image_ref.at[1], t, steps) for t in range(reach)]
    wide = steps + 2 * SEARCH
    sums = row_box(second, wide) + row_box([x * x for x in second], wide)
    sums = jnp.concatenate(parts_of(jnp.concatenate(sums, axis=0)), axis=1)
    stacked = jnp.concatenate(second, axis=0)
    lane = lax.broadcasted_iota(jnp.int32, stacked.shape, 1)
    half = wide * SUB
    for place in range(SIDE):
        shift = place - SEARCH
        moved = pltpu.roll(stacked, (-shift) % columns, 1) if shift else stacked
        inside = (lane + shift >= 0) & (lane + shift < columns)
        s_ref[place] = jnp.where(inside, moved, 0.0).reshape(reach, SUB, columns)
        shifted_band = band_matrix(columns, shift)
        bands = jnp.concatenate([shifted_band] * 3, axis=0)
        boxed = jnp.dot(sums, bands, preferred_element_type=jnp.float32) * AREA
        mean = boxed[:half]
        var = boxed[half:] - mean * mean
        mean_ref[place] = mean.reshape(wide, SUB, columns)
        inv = inverse_root(jnp.maximum(var, VARIANCE_FLOOR))
        inv_ref[place] = inv.reshape(wide, SUB, columns)


def correlate(shift, count, f_ref, s_ref, mean_ref, inv_ref, mean1_ref, inv1_ref, e_ref, side=None, held=None):
    steps, _, columns = mean1_ref.shape
    rows = steps * SUB
    band = band_matrix(columns, 0)
    block = BLOCK if count % BLOCK == 0 else 1

    def body(number, carry):
        sums = []
        for i in range(block):
            k = number * block + i
            oy, ox = shift(k)
            planes = [f_ref[t] * s_ref[ox, oy + t] for t in range(steps + 2 * RADIUS)]
            sums += row_box(planes, steps)
        boxed = column_box(jnp.concatenate(sums, axis=0), band)
        for i in range(block):
            k = number * block + i
            oy, ox = shift(k)
            for t in range(steps):
                at = i * rows + t * SUB
                cov = boxed[at : at + SUB] - mean1_ref[t] * mean_ref[ox, oy + t]
                e_ref[k, t] = jnp.exp(cov * (inv1_ref[t] * inv_ref[ox, oy + t]))
        return carry if side is None else side(number, carry)

    return count // block, lax.fori_loop(0, count // block, body, 0 if side is None else held)


def prior_tables(prior_row, prior_col, a_ref, b_ref, lanes):
    steps = a_ref.shape[1]
    curve = 0.5 * (2.0 * PRIOR_STRENGTH / SOFTMIN_HEAT)
    for t in range(steps):
        for ref, prior in ((a_ref, prior_row(t)), (b_ref, prior_col(t))):
            near = jnp.clip(jnp.floor(prior + 0.5), -float(SEARCH), float(SEARCH))
            twice = near - 2.0 * prior
            for place in range(SIDE):
                i = float(place - SEARCH)
                ref[place, t, :, lanes] = jnp.exp(curve * ((near - i) * (twice + i)))


def match(offsets_ref, e_ref, a_ref, b_ref, lanes, together, store):
    count, steps = e_ref.shape[:2]
    for base in range(0, steps, together):
        here = pl.ds(base, together)
        zero = jnp.zeros((together, SUB, lanes.size), jnp.float32)

        def body(k, carry):
            total, rows, cols = carry
            oy = offsets_ref[k, 0]
            ox = offsets_ref[k, 1]
            table = a_ref[oy + SEARCH, here, :, lanes] * b_ref[ox + SEARCH, here, :, lanes]
            weight = e_ref[k, here, :, lanes] * table
            return (
                total + weight,
                rows + weight * oy.astype(jnp.float32),
                cols + weight * ox.astype(jnp.float32),
            )

        total, rows, cols = lax.fori_loop(0, count, body, (zero, zero, zero), unroll=8)
        for i in range(together):
            store(base + i, rows[i] / total[i], cols[i] / total[i])


def match_cells(cell, e_ref, a_ref, b_ref, lanes, together, store):
    steps = e_ref.shape[1]
    for base in range(0, steps, together):
        here = pl.ds(base, together)
        zero = jnp.zeros((together, SUB, lanes.size), jnp.float32)
        table = [b_ref[j, here, :, lanes] for j in range(SIDE)]
        moment = [x * float(j - SEARCH) for j, x in enumerate(table)]

        def body(i, carry):
            total, rows, cols = carry
            first, second = zero, zero
            for j in range(SIDE):
                e = e_ref[cell(i * SIDE + j), here, :, lanes]
                first = first + e * table[j]
                if j != SEARCH:
                    second = second + e * moment[j]
            a = a_ref[i, here, :, lanes]
            weight = a * first
            shift = lax.convert_element_type(i - SEARCH, jnp.float32)
            return total + weight, rows + weight * shift, cols + a * second

        total, rows, cols = lax.fori_loop(0, SIDE, body, (zero, zero, zero), unroll=True)
        for i in range(together):
            store(base + i, rows[i] / total[i], cols[i] / total[i])


def eliminate(j, a):
    row_id = lax.broadcasted_iota(jnp.int32, a.shape, 0)
    col_id = lax.broadcasted_iota(jnp.int32, a.shape, 1)
    on_row = row_id == j
    on_col = col_id == j
    row = jnp.sum(jnp.where(on_row, a, 0.0), axis=0, keepdims=True)
    col = jnp.sum(jnp.where(on_col, a, 0.0), axis=1, keepdims=True)
    pivot = jnp.sum(jnp.where(col_id[:1] == j, row, 0.0), axis=1, keepdims=True)
    scale = jnp.where(j < a.shape[0], 1.0 / pivot, 0.0)
    inner = a - col * (row * scale)
    return jnp.where(
        on_row,
        jnp.where(on_col, scale, row * scale),
        jnp.where(on_col, -col * scale, inner),
    )


def design_begin(epochs_ref, slot_ref, ends_ref):
    pairs = slot_ref.shape[0]
    ends = 2 * pairs
    row_id = lax.broadcasted_iota(jnp.int32, (pairs, pairs), 0)
    col_id = lax.broadcasted_iota(jnp.int32, (pairs, pairs), 1)
    end_id = lax.broadcasted_iota(jnp.int32, (ends, pairs), 0)
    end_col = lax.broadcasted_iota(jnp.int32, (ends, pairs), 1)
    seg_id = lax.broadcasted_iota(jnp.int32, (ends, EPOCHS), 0)

    def gather(j, state):
        first_r, after_r, first_c, after_c, mark, mark_e, first_e, after_e = state
        first = epochs_ref[0, slot_ref[j]]
        after = epochs_ref[1, slot_ref[j]]
        if ends_ref is not None:
            ends_ref[0, j] = first
            ends_ref[1, j] = after
        return (
            jnp.where(row_id == j, first, first_r),
            jnp.where(row_id == j, after, after_r),
            jnp.where(col_id == j, first, first_c),
            jnp.where(col_id == j, after, after_c),
            jnp.where(end_id == j, first, jnp.where(end_id == j + pairs, after, mark)),
            jnp.where(seg_id == j, first, jnp.where(seg_id == j + pairs, after, mark_e)),
            jnp.where(end_col == j, first, first_e),
            jnp.where(end_col == j, after, after_e),
        )

    square = jnp.zeros((pairs, pairs), jnp.int32)
    tall = jnp.zeros((ends, pairs), jnp.int32)
    state = (square, square, square, square, tall, jnp.zeros((ends, EPOCHS), jnp.int32), tall, tall)
    first_r, after_r, first_c, after_c, mark, mark_e, first_e, after_e = lax.fori_loop(
        0, pairs, gather, state
    )
    overlap = jnp.maximum(jnp.minimum(after_r, after_c) - jnp.maximum(first_r, first_c), 0)
    matrix = overlap.astype(jnp.float32) + jnp.where(row_id == col_id, PENALTY, 0.0)

    inside = ((mark >= first_e) & (mark < after_e)).astype(jnp.float32)
    return matrix, (inside, mark_e)


def design_end(inverse, intervals, coef_ref, seg_ref, weigh=False):
    inside, mark_e = intervals
    ends = inside.shape[0]
    seg_id = lax.broadcasted_iota(jnp.int32, (ends, EPOCHS), 0)
    epoch = lax.broadcasted_iota(jnp.int32, (ends, EPOCHS), 1)
    latest = jnp.max(jnp.where(mark_e <= epoch, mark_e, -1), axis=0, keepdims=True)
    which = jnp.max(jnp.where(mark_e == latest, seg_id, -1), axis=0, keepdims=True)
    which = jnp.where(latest < 0, ends, which)
    seg_ref[0:1] = which
    coef = jnp.dot(inside, inverse, precision=HIGHEST, preferred_element_type=jnp.float32)
    if weigh:
        long = jnp.sum((which == seg_id).astype(jnp.float32), axis=1, keepdims=True)
        blank = jnp.zeros((ends, coef_ref.shape[1] - ends), jnp.float32)
        coef = jnp.concatenate([coef, inside * long, blank], axis=1)
    coef_ref[...] = coef


def design_kernel(epochs_ref, slot_ref, coef_ref, seg_ref, ends_ref):
    matrix, intervals = design_begin(epochs_ref, slot_ref, ends_ref)
    inverse = lax.fori_loop(0, slot_ref.shape[0], eliminate, matrix)
    design_end(inverse, intervals, coef_ref, seg_ref)


def design(pair_epochs, pair_slot):
    pairs = pair_slot.shape[0]
    return pl.pallas_call(
        design_kernel,
        out_shape=(
            jax.ShapeDtypeStruct((2 * pairs, pairs), jnp.float32),
            jax.ShapeDtypeStruct((1, EPOCHS), jnp.int32),
            jax.ShapeDtypeStruct((2, pairs), jnp.int32),
        ),
        in_specs=[smem_spec(), smem_spec()],
        out_specs=(vmem_spec(), vmem_spec(), smem_spec()),
        compiler_params=params(),
        name="design",
    )(pair_epochs.T, pair_slot)


def invert(coef_ref, seg_ref, ends_ref, pairs, d, begin, z, g, t_ref, cum_ref, predict):
    ends = 2 * pairs
    threshold = SPARSITY / PENALTY
    zero = jnp.zeros(t_ref.shape[1:], jnp.float32)
    t_ref[ends] = zero
    cum_ref[0] = zero
    if predict is not None:
        predict[1][0] = zero
    short = pairs <= 16

    for iteration in range(ITERS):
        start = begin is None and iteration == 0
        z_from, g_from = begin if begin and iteration == 0 else (z[0], g[0])
        last = iteration + 1 == ITERS
        summing = last and predict is not None

        def residual(p):
            return d(p) if start else d(p) - g_from(p)

        if short:
            gaps = [residual(p) for p in range(pairs)]
            for j in range(ends):
                value = coef_ref[j, 0] * gaps[0]
                for p in range(1, pairs):
                    value = value + coef_ref[j, p] * gaps[p]
                t_ref[j] = value
        else:

            def fill(j):
                t_ref[j] = lax.fori_loop(
                    0, pairs, lambda p, v: v + coef_ref[j, p] * residual(p), zero
                )

            pl.loop(0, ends)(fill)

        def epoch_step(e, carry):
            s = t_ref[seg_ref[0, e]]
            if not start:
                s = s + z_from(e)
            u = jnp.clip(s, -threshold, threshold)
            new = s - u
            z[1](e, new, last)
            if last and not summing:
                return carry
            run = carry[0] + (new - u)
            cum_ref[e + 1] = run
            if not summing:
                return (run,)
            run_z = carry[1] + new
            predict[1][e + 1] = run_z
            return (run, run_z)

        lax.fori_loop(0, EPOCHS, epoch_step, (zero, zero) if summing else (zero,), unroll=8)
        if last and not summing:
            return

        def collect(p):
            first, after = ends_ref[0, p], ends_ref[1, p]
            g[1](p, cum_ref[after] - cum_ref[first])
            if summing:
                predict[0](p, predict[1][after] - predict[1][first])

        if short:
            for p in range(pairs):
                collect(p)
        else:
            pl.loop(0, pairs)(collect)


def invert_segments(coef_ref, pairs, d, z_ref, g_ref, fresh):
    ends = 2 * pairs
    threshold = SPARSITY / PENALTY
    zero = jnp.zeros(z_ref.shape[1:], jnp.float32)
    if fresh:
        for j in range(ends + 1):
            z_ref[j] = zero
    seen = [d(p) for p in range(pairs)]

    def weigh(j, value, sums):
        return tuple(g + coef_ref[j, pairs + p] * value for p, g in enumerate(sums))

    def step(iteration, held):
        gaps = [a - b for a, b in zip(seen, held)]
        sums = (zero,) * pairs
        for j in range(ends):
            terms = [coef_ref[j, p] * gap for p, gap in enumerate(gaps)]
            while len(terms) > 1:
                terms = [sum(terms[i : i + 2][1:], terms[i]) for i in range(0, len(terms), 2)]
            s = z_ref[j] + terms[0]
            u = jnp.clip(s, -threshold, threshold)
            z = s - u
            z_ref[j] = z
            sums = weigh(j, z - u, sums)
        return sums

    held = (zero,) * pairs if fresh else tuple(g_ref[p] for p in range(pairs))
    held = lax.fori_loop(0, ITERS, step, held)
    if not fresh:
        return None
    for p in range(pairs):
        g_ref[p] = held[p]
    sums = (zero,) * pairs
    for j in range(ends):
        sums = weigh(j, z_ref[j], sums)
    return sums


def second_axis(ref):
    def store(i, value, last=False):
        ref[:, i] = value

    return (lambda i: ref[:, i]), store


def match_scratch(steps, columns):
    plane = (SUB, columns)
    extended = (2, columns // LANES, steps * SUB + 2 * MARGIN, LANES)
    return [
        pltpu.VMEM(extended, jnp.float32),
        pltpu.VMEM((steps + 2 * RADIUS,) + plane, jnp.float32),
        pltpu.VMEM((SIDE, steps + 2 * MARGIN) + plane, jnp.float32),
        pltpu.VMEM((SIDE, steps + 2 * SEARCH) + plane, jnp.float32),
        pltpu.VMEM((SIDE, steps + 2 * SEARCH) + plane, jnp.float32),
        pltpu.VMEM((steps,) + plane, jnp.float32),
        pltpu.VMEM((steps,) + plane, jnp.float32),
    ]


def weight_scratch(steps, columns):
    tables = [pltpu.VMEM((SIDE, steps, SUB, columns), jnp.float32)] * 2
    return tables + [pltpu.VMEM((2, columns // LANES, steps * SUB, LANES), jnp.float32)]


def match_on(offsets_ref, e_ref, prior_ref, back_ref, a_ref, b_ref, field_ref, motion_ref):
    steps = e_ref.shape[1]
    for component in range(2):
        values = prior_ref[component]
        if back_ref is not None:
            values = 0.5 * (values + back_ref[component])
        field_ref[component] = split_lanes(values)

    def prior(component):
        return lambda t: strided(field_ref.at[component], t, steps)

    def store(t, row, col):
        store_strided(field_ref.at[0], t, steps, row)
        store_strided(field_ref.at[1], t, steps, col)

    lanes = pl.ds(0, e_ref.shape[3])
    prior_tables(prior(0), prior(1), a_ref, b_ref, lanes)
    match(offsets_ref, e_ref, a_ref, b_ref, lanes, 2, store)
    for component in range(2):
        halves = [field_ref[component, i] for i in range(field_ref.shape[1])]
        motion_ref[component] = jnp.concatenate(halves, axis=-1)


def first_kernel(offsets_ref, images_ref, prior_ref, e_ref, motion_ref, *scratch):
    image_ref, *tables = scratch[:7]
    for i in range(2):
        image_ref[i] = split_lanes(images_ref[i])
    prepare(image_ref, *tables)
    shift = lambda k: (offsets_ref[k, 0] + SEARCH, offsets_ref[k, 1] + SEARCH)
    correlate(shift, offsets_ref.shape[0], *tables, e_ref)
    match_on(offsets_ref, e_ref, prior_ref, None, *scratch[7:], motion_ref)


def again_kernel(offsets_ref, e_ref, prior_ref, back_ref, motion_ref, *scratch):
    match_on(offsets_ref, e_ref, prior_ref, back_ref, *scratch, motion_ref)


def invert_first_kernel(coef_ref, seg_ref, ends_ref, d_ref, z_ref, g_ref, gz_ref, t_ref, cum_ref, cumz_ref):
    z, g, d, gz = (second_axis(ref) for ref in (z_ref, g_ref, d_ref, gz_ref))
    tables = (coef_ref, seg_ref, ends_ref, d_ref.shape[1])
    invert(*tables, d[0], None, z, g, t_ref, cum_ref, (gz[1], cumz_ref))


def invert_last_kernel(coef_ref, seg_ref, ends_ref, d_ref, zin_ref, gin_ref, z_ref, g_ref, t_ref, cum_ref):
    z, g, d = (second_axis(ref) for ref in (z_ref, g_ref, d_ref))
    begin = (second_axis(zin_ref)[0], second_axis(gin_ref)[0])
    tables = (coef_ref, seg_ref, ends_ref, d_ref.shape[1])
    invert(*tables, d[0], begin, z, g, t_ref, cum_ref, None)


def fused_kernel(
    offsets_hbm,
    epochs_hbm,
    slot_hbm,
    first_hbm,
    second_hbm,
    prior_hbm,
    out_ref,
    index_vmem,
    motion_ref,
    image_ref,
    f_ref,
    s_ref,
    mean_ref,
    inv_ref,
    mean1_ref,
    inv1_ref,
    a_ref,
    b_ref,
    field_ref,
    e_ref,
    prior_ref,
    back_ref,
    d_ref,
    gz_ref,
    z_ref,
    g_ref,
    coef_vmem,
    coef_ref,
    index_ref,
    offsets_ref,
    epochs_ref,
    slot_ref,
    load_sem,
    table_sem,
    halo_sem,
    send_sem,
    recv_sem,
):
    rows, columns = first_hbm.shape
    steps = rows // SUB
    halves = columns // LANES
    pairs = slot_ref.shape[0]
    part = rows // pairs
    count = offsets_ref.shape[1]
    me = lax.axis_index("pairs")
    band = lax.axis_index("rows")
    mesh_id = pl.DeviceIdType.MESH

    barrier = pltpu.get_barrier_semaphore()
    peers = [lax.rem(me + i, pairs) for i in range(1, pairs)]
    pl.semaphore_signal(barrier, inc=1, device_id={"rows": 1 - band}, device_id_type=mesh_id)
    for peer in peers:
        pl.semaphore_signal(barrier, inc=1, device_id={"pairs": peer}, device_id_type=mesh_id)

    moves = [(epochs_hbm, epochs_ref), (slot_hbm, slot_ref), (offsets_hbm, offsets_ref)]
    for half in range(halves):
        lanes = pl.ds(half * LANES, LANES)
        inner = pl.ds(MARGIN, rows)
        moves += [
            (prior_hbm.at[0, :, lanes], prior_ref.at[0, half]),
            (prior_hbm.at[1, :, lanes], prior_ref.at[1, half]),
            (first_hbm.at[:, lanes], image_ref.at[0, half, inner]),
            (second_hbm.at[:, lanes], image_ref.at[1, half, inner]),
        ]
    loads = [
        pltpu.make_async_copy(source, target, load_sem.at[i])
        for i, (source, target) in enumerate(moves)
    ]
    for load in loads:
        load.start()
    outer = pl.ds(pl.multiple_of(band * (rows + MARGIN), SUB), MARGIN)
    edge = pl.ds(pl.multiple_of((1 - band) * (rows - MARGIN), SUB), MARGIN)
    image_ref[:, :, outer, :] = jnp.zeros((2, halves, MARGIN, LANES), jnp.float32)
    pl.semaphore_wait(barrier, pairs)
    halos = []
    for i, source in enumerate((first_hbm, second_hbm)):
        for half in range(halves):
            halo = pltpu.make_async_remote_copy(
                src_ref=source.at[edge, pl.ds(half * LANES, LANES)],
                dst_ref=image_ref.at[i, half, outer, :],
                send_sem=halo_sem.at[0, i, half],
                recv_sem=halo_sem.at[1, i, half],
                device_id={"rows": 1 - band},
                device_id_type=mesh_id,
            )
            halo.start()
            halos.append(halo)

    for load in loads[:3]:
        load.wait()
    index_vmem[...] = jnp.zeros(index_vmem.shape, jnp.int32)
    matrix, intervals = design_begin(epochs_ref, slot_ref, None)
    lane = lax.broadcasted_iota(jnp.int32, (1, LANES), 1)

    def place(k, held):
        cell = (offsets_ref[0, k] + SEARCH) * SIDE + offsets_ref[1, k] + SEARCH
        return jnp.where(lane == cell, k, held)

    index_vmem[1:2] = lax.fori_loop(0, count, place, jnp.full((1, LANES), count, jnp.int32), unroll=8)
    e_ref[count] = jnp.zeros(e_ref.shape[1:], jnp.float32)
    for load in loads[3:]:
        load.wait()
    prior_tables(
        lambda t: strided(prior_ref.at[0], t, steps),
        lambda t: strided(prior_ref.at[1], t, steps),
        a_ref,
        b_ref,
        pl.ds(0, columns),
    )
    for halo in halos:
        halo.wait()
    prepare(image_ref, f_ref, s_ref, mean_ref, inv_ref, mean1_ref, inv1_ref)
    shift = lambda k: (offsets_ref[0, k] + SEARCH, offsets_ref[1, k] + SEARCH)
    images = (f_ref, s_ref, mean_ref, inv_ref, mean1_ref, inv1_ref)
    done, matrix = correlate(shift, count, *images, e_ref, eliminate, matrix)
    inverse = lax.fori_loop(done, max(done, pairs), eliminate, matrix) if done < pairs else matrix
    design_end(inverse, intervals, coef_vmem, index_vmem, True)
    tables = [
        pltpu.make_async_copy(coef_vmem, coef_ref, table_sem.at[0]),
        pltpu.make_async_copy(index_vmem, index_ref, table_sem.at[1]),
    ]
    for move in tables:
        move.start()
    for move in tables:
        move.wait()

    def block(index):
        return pl.ds(pl.multiple_of(index * part, SUB), part)

    def push(phase, half, source, target):
        copies = []
        for i, peer in enumerate(peers):
            copy = pltpu.make_async_remote_copy(
                src_ref=source(peer),
                dst_ref=target(me),
                send_sem=send_sem.at[phase, half, i],
                recv_sem=recv_sem.at[phase, half, i],
                device_id={"pairs": peer},
                device_id_type=mesh_id,
            )
            copy.start()
            copies.append(copy)
        target(me)[...] = source(me)[...]
        return copies

    def finish(copies):
        for copy in copies:
            copy.wait()

    def match_half(phase, half):
        lanes = pl.ds(half * LANES, LANES)

        def store(t, row, col):
            field_ref[0, half, pl.ds(t, SUB, stride=steps), :] = row
            field_ref[1, half, pl.ds(t, SUB, stride=steps), :] = col

        cell = lambda i: index_ref[1, i]
        match_cells(cell, e_ref, a_ref, b_ref, lanes, 2 if steps % 2 == 0 else 1, store)
        return push(
            phase,
            half,
            lambda q: field_ref.at[:, half, block(q), :],
            lambda q: d_ref.at[phase // 2, half, q],
        )

    def invert_half(phase, half):
        sums = invert_segments(
            coef_ref,
            pairs,
            lambda p: d_ref[phase // 2, half, p],
            z_ref.at[half],
            g_ref.at[half],
            phase == 0,
        )
        if phase == 0:
            for p in range(pairs):
                gz_ref[half, p] = sums[p]
            return
        for segment in range(2 * pairs + 1):
            for component in range(2):
                out_ref[segment, component, pl.ds(half, part, stride=halves), :] = z_ref[
                    half, segment, component
                ]

    sent = [match_half(0, half) for half in range(halves)]
    returned = []
    for half in range(halves):
        finish(sent[half])
        invert_half(0, half)
        returned.append(
            push(
                1,
                half,
                lambda q: gz_ref.at[half, q],
                lambda q: back_ref.at[:, half, block(q), :],
            )
        )
    sent = []
    for half in range(halves):
        finish(returned[half])

        def prior(component):
            def at(t):
                place = pl.ds(t, SUB, stride=steps)
                given = prior_ref[component, half, place, :]
                return 0.5 * (given + back_ref[component, half, place, :])

            return at

        prior_tables(prior(0), prior(1), a_ref, b_ref, pl.ds(half * LANES, LANES))
        sent.append(match_half(2, half))
    for component in range(2):
        pieces = [field_ref[component, half] for half in range(halves)]
        motion_ref[component] = jnp.concatenate(pieces, axis=-1)
    for half in range(halves):
        finish(sent[half])
        invert_half(2, half)


def expand_kernel(z_hbm, index_hbm, motion_hbm, velocity_hbm, out_hbm, z_ref, index_ref, velocity_ref, sem, out_sem):
    moves = [
        pltpu.make_async_copy(z_hbm, z_ref, sem.at[0]),
        pltpu.make_async_copy(index_hbm, index_ref, sem.at[1]),
        pltpu.make_async_copy(motion_hbm, out_hbm, sem.at[2]),
    ]
    for move in moves:
        move.start()
    moves[0].wait()
    moves[1].wait()
    length = EPOCHS // PIECES
    outs = []
    for piece in range(PIECES):

        def expand(i, carry):
            e = piece * length + i
            velocity_ref[:, e] = z_ref[index_ref[0, e]]
            return carry

        lax.fori_loop(0, length, expand, 0, unroll=8)
        for component in range(2):
            here = (component, pl.ds(piece * length, length))
            out = pltpu.make_async_copy(
                velocity_ref.at[here], velocity_hbm.at[here], out_sem.at[component, piece]
            )
            out.start()
            outs.append(out)
    for out in outs:
        out.wait()
    moves[2].wait()


def fused(first_image, second_image, prior, offsets, pair_epochs, pair_slot):
    rows, columns = first_image.shape
    steps, halves = rows // SUB, columns // LANES
    count, pairs = offsets.shape[0], pair_slot.shape[0]
    part = rows // pairs
    f32, i32 = jnp.float32, jnp.int32
    plane = (2, part, LANES)
    split = (2, halves, rows, LANES)
    dma = pltpu.SemaphoreType.DMA
    z, index, motion = pl.pallas_call(
        fused_kernel,
        out_shape=(
            jax.ShapeDtypeStruct((2 * pairs + 1, 2, part * halves, LANES), f32),
            jax.ShapeDtypeStruct((SUB, EPOCHS), i32),
            jax.ShapeDtypeStruct((2, rows, columns), f32),
        ),
        in_specs=[hbm_spec()] * 6,
        out_specs=(vmem_spec(),) * 3,
        scratch_shapes=match_scratch(steps, columns)
        + weight_scratch(steps, columns)
        + [
            pltpu.VMEM((count + 1, steps, SUB, columns), f32),
            pltpu.VMEM(split, f32),
            pltpu.VMEM(split, f32),
            pltpu.VMEM((ROUNDS, halves, pairs) + plane, f32),
            pltpu.VMEM((halves, pairs) + plane, f32),
            pltpu.VMEM((halves, 2 * pairs + 1) + plane, f32),
            pltpu.VMEM((halves, pairs) + plane, f32),
            pltpu.VMEM((2 * pairs, LANES), f32),
            pltpu.SMEM((2 * pairs, LANES), f32),
            pltpu.SMEM((SUB, EPOCHS), i32),
            pltpu.SMEM((2, count), i32),
            pltpu.SMEM((2, pairs), i32),
            pltpu.SMEM((pairs,), i32),
            dma((3 + 4 * halves,)),
            dma((2,)),
            dma((2, 2, halves)),
            dma((3, halves, pairs)),
            dma((3, halves, pairs)),
        ],
        compiler_params=params(collective_id=0, has_side_effects=True),
        name="track",
    )(offsets.T, pair_epochs.T, pair_slot, first_image, second_image, prior)
    whole = (2, EPOCHS, part * halves, LANES)
    return pl.pallas_call(
        expand_kernel,
        out_shape=(
            jax.ShapeDtypeStruct(whole, f32),
            jax.ShapeDtypeStruct((2, rows, columns), f32),
        ),
        in_specs=[hbm_spec()] * 3,
        out_specs=(hbm_spec(),) * 2,
        scratch_shapes=[
            pltpu.VMEM(z.shape, f32),
            pltpu.SMEM(index.shape, i32),
            pltpu.VMEM(whole, f32),
            dma((3,)),
            dma((2, PIECES)),
        ],
        compiler_params=params(),
        name="expand",
    )(z, index, motion)


def with_halo(cells, axis, dim, width):
    count = lax.axis_size(axis)
    head = lax.slice_in_dim(cells, 0, width, axis=dim)
    tail = lax.slice_in_dim(cells, cells.shape[dim] - width, cells.shape[dim], axis=dim)
    down = lax.ppermute(tail, axis, [(i, i + 1) for i in range(count - 1)])
    up = lax.ppermute(head, axis, [(i + 1, i) for i in range(count - 1)])
    return jnp.concatenate([down, cells, up], axis=dim)


def per_device(first_image, second_image, prior_motion, offsets, pair_epochs, pair_slot):
    rows, columns = first_image.shape[1:]
    steps = rows // SUB
    pairs = lax.axis_size("pairs")
    pixels = rows * columns // pairs
    fold = (pixels // LANES, LANES) if pixels % LANES == 0 else (1, pixels)
    f32 = functools.partial(jax.ShapeDtypeStruct, dtype=jnp.float32)
    prior = prior_motion[:, 0]
    whole_tiles = rows % (SUB * pairs) == 0 and columns % LANES == 0 and 2 * pairs <= LANES
    if whole_tiles and lax.axis_size("rows") == 2:
        velocity, motion = fused(
            first_image[0], second_image[0], prior, offsets, pair_epochs, pair_slot
        )
        return (velocity.reshape(2, EPOCHS, 1, pixels), motion[:, None])
    coef, seg, ends = design(pair_epochs, pair_slot)
    images = with_halo(jnp.concatenate((first_image, second_image), axis=0), "rows", 1, MARGIN)
    e, motion = pl.pallas_call(
        first_kernel,
        out_shape=(f32((offsets.shape[0], steps, SUB, columns)), f32((2, rows, columns))),
        in_specs=[smem_spec(), vmem_spec(), vmem_spec()],
        out_specs=(vmem_spec(), vmem_spec()),
        scratch_shapes=match_scratch(steps, columns) + weight_scratch(steps, columns),
        compiler_params=params(),
        name="correlate",
    )(offsets, images, prior)

    def spread(field):
        outgoing = field.reshape(2, 1, pairs, pixels)
        arrived = lax.all_to_all(outgoing, "pairs", split_axis=2, concat_axis=1, tiled=True)
        return arrived.reshape((2, pairs) + fold)

    def collect(field):
        outgoing = field.reshape(2, pairs, 1, pixels)
        arrived = lax.all_to_all(outgoing, "pairs", split_axis=1, concat_axis=2, tiled=True)
        return arrived.reshape(2, rows, columns)

    z_shape, g_shape = f32((2, EPOCHS) + fold), f32((2, pairs) + fold)
    tables = [
        pltpu.VMEM((2 * pairs + 1, 2) + fold, jnp.float32),
        pltpu.VMEM((EPOCHS + 1, 2) + fold, jnp.float32),
    ]
    small = [smem_spec()] * 3
    z, g, predicted = pl.pallas_call(
        invert_first_kernel,
        out_shape=(z_shape, g_shape, g_shape),
        in_specs=small + [vmem_spec()],
        out_specs=(vmem_spec(),) * 3,
        scratch_shapes=tables + [tables[1]],
        compiler_params=params(),
        name="invert_first",
    )(coef, seg, ends, spread(motion))
    motion = pl.pallas_call(
        again_kernel,
        out_shape=f32((2, rows, columns)),
        in_specs=[smem_spec()] + [vmem_spec()] * 3,
        out_specs=vmem_spec(),
        scratch_shapes=weight_scratch(steps, columns),
        compiler_params=params(),
        name="match_again",
    )(offsets, e, prior, collect(predicted))
    z, g = pl.pallas_call(
        invert_last_kernel,
        out_shape=(z_shape, g_shape),
        in_specs=small + [vmem_spec()] * 3,
        out_specs=(vmem_spec(),) * 2,
        scratch_shapes=tables,
        compiler_params=params(),
        name="invert_last",
    )(coef, seg, ends, spread(motion), z, g)
    return (z.reshape(2, EPOCHS, 1, pixels), motion[:, None])


def solution(mesh):
    placed = (
        P(("groups", "pairs"), "rows", None),
        P(("groups", "pairs"), "rows", None),
        P(None, ("groups", "pairs"), "rows", None),
        P(),
        P("groups", None),
        P("groups"),
    )
    return jax.shard_map(
        per_device,
        mesh=mesh,
        in_specs=placed,
        out_specs=(
            P(None, None, ("groups", "rows"), "pairs"),
            P(None, ("groups", "pairs"), "rows", None),
        ),
        check_vma=False,
    )
```
